32 devices in a mesh: req: 2 (over x), tile: 16 (over z, y, core).
Axes of the slice: x: 2, y: 2, z: 4, core: 2. Of those that a mesh axis runs over, the one named last changes fastest.
Arguments:
- queries: bfloat16 [32, 512, 384], P(('req', 'tile')), parts along dimension 0, may hold values from -12 to 12
- keys: bfloat16 [32, 512, 384], P(('req', 'tile')), parts along dimension 0, may hold values from -5 to 5
- values: bfloat16 [32, 512, 384], P(('req', 'tile')), parts along dimension 0, may hold values from -6 to 6
- text_keys: bfloat16 [512, 1536], P(('req', 'tile')), parts along dimension 0, may hold values from -6 to 6
- text_values: bfloat16 [512, 1536], P(('req', 'tile')), parts along dimension 0, may hold values from -6 to 6
- text_mask: int32 [512], P(('req', 'tile')), parts along dimension 0, may hold values 0 or 1
Outputs:
- attended: bfloat16 [32, 512, 384], P(('req', 'tile')), parts along dimension 0
The draws below stay inside these ranges and needn't reach their ends.
There are 2 independent parts, one for each index of `req`. The reference program is written for one: setup_inputs(seed, part) draws one part's arguments, and reference() takes and returns one part's arrays. A program takes and returns all parts, laid end to end along the dimension named above; each array names one. Nothing has to cross between parts.
All inputs are finite; a program needn't handle non-finite values. No bound on the sum of `text_mask` on one device may be relied on, other than what follows from the above.
Results may differ from the reference program's by a relative error of at most 0.004.
Values may be sent and summed in bfloat16 or wider, within the bound.
A program may use at most 192 MiB of HBM per device.

```python
import math
import jax
import jax.numpy as jnp
from jax import lax

TS = 8
HEADS = 12
HEAD_DIM = 128
HEAD_GROUPS = 4
TEXT = 256
TT = 512
HEADS_DEV = 3
WIDTH_DEV = 384
TILES = 4
GW = 4
GH = 1
GF = 1
VALID_FRAMES = 6


def draw_queries(key, part):
    full_shape = (TILES * HEAD_GROUPS, TT, HEADS_DEV * HEAD_DIM)
    base_key = jax.random.fold_in(key, 3)
    drawn = jnp.clip(2.8 * jax.random.normal(base_key, full_shape, jnp.float32), -12.0, 12.0)
    return drawn.astype(jnp.bfloat16)


def draw_keys(key, part):
    full_shape = (TILES * HEAD_GROUPS, TT, HEADS_DEV * HEAD_DIM)
    base_key = jax.random.fold_in(key, 5)
    drawn = jnp.clip(jax.random.normal(base_key, full_shape, jnp.float32), -5.0, 5.0)
    return drawn.astype(jnp.bfloat16)


def set_ends(values, key, least, largest):
    shape = values.shape
    index_at = [jax.random.randint(jax.random.fold_in(key, axis), (), 0, shape[axis]) for axis in range(len(shape))]
    values = values.at[tuple(index_at)].set(least)
    longest = shape.index(max(shape))
    index_at[longest] = (index_at[longest] + 1) % shape[longest]
    return values.at[tuple(index_at)].set(largest)


def block_scale(rng, dims, split, low, top_value):
    factor_of = 1.0
    for dim, blocks in split:
        draws = jax.random.uniform(jax.random.fold_in(jax.random.fold_in(rng, 6), dim), (blocks,), jnp.float32, low / len(split), top_value / len(split))
        factor_of = factor_of * jnp.repeat(jnp.exp(draws), dims[dim] // blocks).reshape((-1,) + (1,) * (len(dims) - 1 - dim))
    return factor_of


def bell_draw(key, shape, deviation, bound, pieces=(), kind=jnp.bfloat16):
    entries = jax.random.normal(key, shape, jnp.float32) * deviation
    if len(pieces) > 0:
        entries = block_scale(key, shape, pieces, -0.22, 0.18) * entries
    return jnp.clip(entries, min=-bound, max=bound).astype(kind)


def setup_inputs(seed: int = 0, part: int = 0) -> dict:
    splits = jax.random.split(jax.random.key(seed), 7)
    part_splits = jax.random.split(jax.random.fold_in(splits[6], part), 7)
    return {
        "queries": draw_queries(jax.random.fold_in(jax.random.fold_in(splits[6], part), 71), part),
        "keys": draw_keys(jax.random.fold_in(jax.random.fold_in(splits[6], part), 71), part),
        "values": bell_draw(part_splits[2], (TILES * HEAD_GROUPS, TT, WIDTH_DEV), 1.0, 6.0, ((0, 16),)),
        "text_keys": bell_draw(part_splits[3], (TEXT, HEADS * HEAD_DIM), 1.0, 6.0, ((0, 16),)),
        "text_values": bell_draw(part_splits[4], (TEXT, HEADS * HEAD_DIM), 1.0, 6.0, ((0, 16),)),
        "text_mask": set_ends((jax.random.randint(part_splits[5], (TEXT,), 0, 4) < 3).astype(jnp.int32), jax.random.fold_in(part_splits[5], 1), 0, 1),
    }


MASKED = -1e+30

def reference(queries, keys, values, text_keys, text_values, text_mask):
    lane_width = HEADS_DEV * HEAD_DIM
    score_scale = 1.0 / math.sqrt(HEAD_DIM)
    grid_keys = keys.reshape(GF, GH, GW, HEAD_GROUPS, TT, lane_width)
    grid_values = values.reshape(GF, GH, GW, HEAD_GROUPS, TT, lane_width)
    pad_spec = ((1, 1), (1, 1), (1, 1), (0, 0), (0, 0), (0, 0))
    padded_keys = jnp.pad(grid_keys, pad_spec)
    padded_values = jnp.pad(grid_values, pad_spec)
    frame_local = jnp.arange(TT, dtype=jnp.int32) // (TS * TS)
    text_keep = text_mask > 0

    def one_block(block_id):
        tile_id = block_id // HEAD_GROUPS
        head_group = block_id % HEAD_GROUPS
        w_pos = tile_id % GW
        h_pos = tile_id // GW % GH
        f_pos = tile_id // (GW * GH)
        zero_index = jnp.zeros((), jnp.int32)
        corner = (f_pos.astype(jnp.int32), h_pos.astype(jnp.int32), w_pos.astype(jnp.int32), head_group.astype(jnp.int32), zero_index, zero_index)
        near_keys = lax.dynamic_slice(padded_keys, corner, (3, 3, 3, 1, TT, lane_width)).reshape(27 * TT, lane_width)
        near_values = lax.dynamic_slice(padded_values, corner, (3, 3, 3, 1, TT, lane_width)).reshape(27 * TT, lane_width)
        offsets = jnp.arange(3, dtype=jnp.int32) - 1
        f_near = f_pos + offsets
        h_near = h_pos + offsets
        w_near = w_pos + offsets
        f_inside = (f_near >= 0) & (f_near < GF)
        h_inside = (h_near >= 0) & (h_near < GH)
        w_inside = (w_near >= 0) & (w_near < GW)
        frame_ok = f_near[:, None] * TS + frame_local[None, :] < VALID_FRAMES
        key_keep = f_inside[:, None, None, None] & h_inside[None, :, None, None] & w_inside[None, None, :, None] & frame_ok[:, None, None, :]
        key_keep = jnp.concatenate([key_keep.reshape(-1), text_keep], axis=0)
        text_cols = lax.dynamic_slice_in_dim(text_keys, (head_group * lane_width).astype(jnp.int32), lane_width, 1)
        text_vals = lax.dynamic_slice_in_dim(text_values, (head_group * lane_width).astype(jnp.int32), lane_width, 1)
        all_keys = jnp.concatenate([near_keys, text_cols], axis=0).astype(jnp.float32).reshape(-1, HEADS_DEV, HEAD_DIM)
        all_values = jnp.concatenate([near_values, text_vals], axis=0).astype(jnp.float32).reshape(-1, HEADS_DEV, HEAD_DIM)
        query_rows = queries[block_id].astype(jnp.float32).reshape(TT, HEADS_DEV, HEAD_DIM)
        scores = jnp.einsum('qhd,khd->hqk', query_rows, all_keys) * score_scale
        scores = jnp.where(key_keep[None, None, :], scores, MASKED)
        row_top = lax.optimization_barrier(jnp.max(scores, axis=-1, keepdims=True))
        exp_terms = jnp.where(key_keep[None, None, :], jnp.exp(scores - row_top), 0.0)
        row_total = lax.optimization_barrier(jnp.sum(exp_terms, axis=-1))
        rounded = lax.optimization_barrier(exp_terms.astype(jnp.bfloat16))
        weights = rounded.astype(jnp.float32)
        summed = jnp.einsum('hqk,khd->qhd', weights, all_values)
        result = summed / jnp.transpose(row_total)[:, :, None]
        return result.reshape(TT, lane_width).astype(jnp.bfloat16)
    return lax.map(one_block, jnp.arange(TILES * HEAD_GROUPS, dtype=jnp.int32))
```

```python
import functools
import math

import jax
import jax.numpy as jnp
from jax import lax
from jax.experimental import pallas as pl
from jax.experimental.pallas import tpu as pltpu
from jax.sharding import PartitionSpec as P

MESH = pl.DeviceIdType.MESH
EXP2_SCALE = math.log2(math.e) / math.sqrt(128)

TS = 8
HEAD_DIM = 128
HEAD_GROUPS = 4


MASKED = -1e30


def passed_along(value, axis, steps):
    count = lax.axis_size(axis)
    first, last = (max(0, -steps), min(count, count - steps))
    return lax.ppermute(value, axis, [(source, source + steps) for source in range(first, last)])


def shortened(value):
    return jax.tree.map(lambda a: a.astype(jnp.bfloat16) if a.dtype == jnp.float32 else a, value)


def fold_block(running, query_heads, key_block, value_block, key_keep):
    row_top, row_total, summed = running
    head_count = query_heads.shape[1]
    key_heads = key_block.reshape(key_block.shape[0], head_count, HEAD_DIM)
    value_heads = value_block.reshape(value_block.shape[0], head_count, HEAD_DIM)
    scores = jnp.einsum("qhd,khd->hqk", query_heads, key_heads, preferred_element_type=jnp.float32)
    scores = scores * (1.0 / math.sqrt(HEAD_DIM))
    scores = jnp.where(key_keep[None, None, :], scores, MASKED)
    new_top = jnp.maximum(row_top, jnp.max(scores, axis=-1))
    scale_down = jnp.exp(row_top - new_top)
    exp_terms = jnp.where(key_keep[None, None, :], jnp.exp(scores - new_top[:, :, None]), 0.0)
    row_total = row_total * scale_down + jnp.sum(exp_terms, axis=-1)
    weights = exp_terms.astype(jnp.bfloat16)
    summed = summed * scale_down[:, :, None] + jnp.einsum(
        "hqk,khd->hqd", weights, value_heads, preferred_element_type=jnp.float32
    )
    return (new_top, row_total, summed)


def gathered_shards(queries, keys, values, text_keys, text_values, text_mask):
    tokens = queries.shape[1]
    lane_width = queries.shape[2]
    head_count = lane_width // HEAD_DIM
    query_heads = queries[0].reshape(tokens, head_count, HEAD_DIM)
    own_pair = jnp.stack([keys[0], values[0]])
    group_count = HEAD_GROUPS
    tiles_all = lax.axis_size("tile") // group_count
    grid_w = min(4, tiles_all)
    grid_h = min(4, tiles_all // grid_w)
    grid_f = tiles_all // (grid_w * grid_h)
    frames_valid = grid_f * TS - TS // 4
    my_index = lax.axis_index("tile")
    tile_id = my_index // group_count
    head_group = my_index % group_count
    w_pos = tile_id % grid_w
    h_pos = tile_id // grid_w % grid_h
    f_pos = tile_id // (grid_w * grid_h)
    local_frame = jnp.arange(tokens, dtype=jnp.int32) // (TS * TS)

    def keep_mask(off_frame, off_height, off_width):
        inside = (
            (f_pos + off_frame >= 0)
            & (f_pos + off_frame < grid_f)
            & (h_pos + off_height >= 0)
            & (h_pos + off_height < grid_h)
            & (w_pos + off_width >= 0)
            & (w_pos + off_width < grid_w)
        )
        return inside & ((f_pos + off_frame) * TS + local_frame < frames_valid)

    running = (
        jnp.full((head_count, tokens), MASKED, jnp.float32),
        jnp.zeros((head_count, tokens), jnp.float32),
        jnp.zeros((head_count, tokens, HEAD_DIM), jnp.float32),
    )
    text_flags = text_mask.astype(jnp.bfloat16)
    piece_keys = lax.dynamic_slice_in_dim(
        lax.all_gather(text_keys, "tile", axis=0, tiled=True),
        head_group * lane_width,
        lane_width,
        1,
    )
    piece_values = lax.dynamic_slice_in_dim(
        lax.all_gather(text_values, "tile", axis=0, tiled=True),
        head_group * lane_width,
        lane_width,
        1,
    )
    running = fold_block(
        running,
        query_heads,
        piece_keys,
        piece_values,
        lax.all_gather(text_flags, "tile", axis=0, tiled=True) > 0.5,
    )
    running = fold_block(running, query_heads, own_pair[0], own_pair[1], keep_mask(0, 0, 0))
    width_set = {0: own_pair}
    for off_width in (-1, 1):
        width_set[off_width] = passed_along(own_pair, "tile", -off_width * group_count)
    width_offsets = sorted(width_set)
    row_stack = jnp.stack([width_set[spot] for spot in width_offsets])
    height_set = {0: row_stack}
    if grid_h > 1:
        for off_height in (-1, 1):
            height_set[off_height] = passed_along(
                shortened(row_stack), "tile", -off_height * grid_w * group_count
            ).astype(row_stack.dtype)
    height_offsets = sorted(height_set)
    slab_stack = jnp.stack([height_set[spot] for spot in height_offsets])

    def fold_slab(state_now, slab_pairs, off_frame):
        for h_slot, off_height in enumerate(height_offsets):
            for w_slot, off_width in enumerate(width_offsets):
                if off_frame == 0 and off_height == 0 and (off_width == 0):
                    continue
                state_now = fold_block(
                    state_now,
                    query_heads,
                    slab_pairs[h_slot, w_slot, 0],
                    slab_pairs[h_slot, w_slot, 1],
                    keep_mask(off_frame, off_height, off_width),
                )
        return state_now

    running = fold_slab(running, slab_stack, 0)
    if grid_f > 1:
        for off_frame in (-1, 1):
            got_slab = passed_along(
                shortened(slab_stack), "tile", -off_frame * grid_h * grid_w * group_count
            ).astype(slab_stack.dtype)
            running = fold_slab(running, got_slab, off_frame)
    row_top, row_total, summed = running
    result = summed / row_total[:, :, None]
    result = jnp.transpose(result, (1, 0, 2)).reshape(tokens, lane_width)
    return result.astype(jnp.bfloat16)[None]


def row_kernel(
    count, rows_kept, head_count, text_rows,
    q_hbm, k_hbm, v_hbm, tk_hbm, tv_hbm, mask_ref, out_hbm,
    q_ref, k_ref, v_ref, tk_ref, tv_ref, packets, text, near_k, near_v, out_ref,
    top_ref, total_ref, summed_ref,
    in_sem, out_sem, text_send, text_recv, near_send, near_recv,
):
    groups = HEAD_GROUPS
    width = head_count * HEAD_DIM
    me = lax.axis_index("tile")
    group = lax.rem(me, groups)
    has_left = me >= groups
    has_right = me < count - groups

    barrier = pltpu.get_barrier_semaphore()
    for step in range(1, count):
        pl.semaphore_signal(barrier, inc=1, device_id={"tile": lax.rem(me + step, count)}, device_id_type=MESH)

    loads = [
        pltpu.make_async_copy(tk_hbm, tk_ref, in_sem.at[0]),
        pltpu.make_async_copy(tv_hbm, tv_ref, in_sem.at[1]),
        pltpu.make_async_copy(q_hbm.at[0], q_ref, in_sem.at[2]),
        pltpu.make_async_copy(k_hbm.at[0, pl.ds(0, rows_kept), :], k_ref, in_sem.at[3]),
        pltpu.make_async_copy(v_hbm.at[0, pl.ds(0, rows_kept), :], v_ref, in_sem.at[4]),
    ]
    for load in loads:
        load.start()

    row_of = lax.broadcasted_iota(jnp.int32, (text_rows, HEAD_DIM), 0)
    flags = jnp.zeros((text_rows, HEAD_DIM), jnp.float32)
    for row in range(text_rows):
        flags = jnp.where(row_of == row, mask_ref[row].astype(jnp.float32), flags)
    flags = flags.astype(jnp.bfloat16)
    loads[0].wait()
    loads[1].wait()
    for to in range(groups):
        packets[to, :, 0:width] = tk_ref[:, to * width : (to + 1) * width]
        packets[to, :, width : 2 * width] = tv_ref[:, to * width : (to + 1) * width]
        packets[to, :, 2 * width :] = flags
    my_rows = pl.ds(pl.multiple_of(me * text_rows, text_rows), text_rows)
    text[my_rows, :] = packets[group]

    pl.semaphore_wait(barrier, count - 1)

    def text_copy(step):
        to = lax.rem(me + step, count)
        return pltpu.make_async_remote_copy(
            src_ref=packets.at[lax.rem(to, groups)],
            dst_ref=text.at[my_rows, :],
            send_sem=text_send.at[step],
            recv_sem=text_recv.at[step],
            device_id={"tile": to},
            device_id_type=MESH,
        )

    def near_copies(side, head):
        to = me + groups if side == 0 else me - groups
        cols = pl.ds(head * HEAD_DIM, HEAD_DIM)
        made = []
        for which, (source, target) in enumerate(((k_hbm, near_k), (v_hbm, near_v))):
            made.append(
                pltpu.make_async_remote_copy(
                    src_ref=source.at[0, pl.ds(0, rows_kept), cols],
                    dst_ref=target.at[side, :, cols],
                    send_sem=near_send.at[side, head, which],
                    recv_sem=near_recv.at[side, head, which],
                    device_id={"tile": to},
                    device_id_type=MESH,
                )
            )
        return made

    for step in range(1, count):
        text_copy(step).start()
    for head in range(head_count):
        for side, there in ((0, has_right), (1, has_left)):

            @pl.when(there)
            def _():
                for copy in near_copies(side, head):
                    copy.start()

    def fold(head, keys, values, keep, first):
        query = q_ref[:, head * HEAD_DIM : (head + 1) * HEAD_DIM]
        scores = lax.dot_general(query, keys, (((1,), (1,)), ((), ())), preferred_element_type=jnp.float32)
        if keep is not None:
            scores = jnp.where(keep, scores, MASKED)
        block_top = jnp.broadcast_to(jnp.max(scores, axis=1, keepdims=True), (scores.shape[0], HEAD_DIM))
        new_top = block_top if first else jnp.maximum(top_ref[head], block_top)
        pieces = [
            jnp.exp2((scores[:, at : at + HEAD_DIM] - new_top) * EXP2_SCALE) for at in range(0, keys.shape[0], HEAD_DIM)
        ]
        part = functools.reduce(lambda a, b: a + b, pieces)
        weights = jnp.concatenate([piece.astype(jnp.bfloat16) for piece in pieces], axis=1)
        product = jnp.dot(weights, values, preferred_element_type=jnp.float32)
        if first:
            total_ref[head] = part
            summed_ref[head] = product
        else:
            scale_down = jnp.exp2((top_ref[head] - new_top) * EXP2_SCALE)
            total_ref[head] = total_ref[head] * scale_down + part
            summed_ref[head] = summed_ref[head] * scale_down + product
        top_ref[head] = new_top

    for load in loads[2:]:
        load.wait()
    for head in range(head_count):
        cols = slice(head * HEAD_DIM, (head + 1) * HEAD_DIM)
        fold(head, k_ref[:, cols], v_ref[:, cols], None, True)

    for step in range(1, count):
        text_copy(step).wait_recv()
    lane = lax.broadcasted_iota(jnp.int32, (8, HEAD_DIM), 1)
    pick = jnp.where(lane == 0, 1.0, 0.0).astype(jnp.bfloat16)
    keep_row = lax.dot_general(
        pick, text[:, 2 * width :], (((1,), (1,)), ((), ())), preferred_element_type=jnp.float32
    )[0:1, :]
    keep = jnp.broadcast_to(keep_row, (q_ref.shape[0], keep_row.shape[1])) > 0.5
    for head in range(head_count):
        at = head * HEAD_DIM
        fold(head, text[:, at : at + HEAD_DIM], text[:, width + at : width + at + HEAD_DIM], keep, False)

    for head in range(head_count):
        cols = slice(head * HEAD_DIM, (head + 1) * HEAD_DIM)
        for side, there in ((0, has_left), (1, has_right)):

            @pl.when(there)
            def _():
                for copy in near_copies(side, head):
                    copy.wait_recv()
                fold(head, near_k[side, :, cols], near_v[side, :, cols], None, False)

        total = jnp.sum(total_ref[head], axis=1, keepdims=True)
        out_ref[:, cols] = (summed_ref[head] / total).astype(out_ref.dtype)
        pltpu.make_async_copy(
            out_ref.at[:, pl.ds(head * HEAD_DIM, HEAD_DIM)],
            out_hbm.at[0, :, pl.ds(head * HEAD_DIM, HEAD_DIM)],
            out_sem.at[head],
        ).start()

    for step in range(1, count):
        text_copy(step).wait_send()
    for head in range(head_count):
        for side, there in ((0, has_right), (1, has_left)):

            @pl.when(there)
            def _():
                for copy in near_copies(side, head):
                    copy.wait_send()

    for head in range(head_count):
        pltpu.make_async_copy(
            out_ref.at[:, pl.ds(head * HEAD_DIM, HEAD_DIM)],
            out_hbm.at[0, :, pl.ds(head * HEAD_DIM, HEAD_DIM)],
            out_sem.at[head],
        ).wait()


def row_shards(queries, keys, values, text_keys, text_values, text_mask):
    tokens, width = queries.shape[1:]
    head_count = width // HEAD_DIM
    count = lax.axis_size("tile")
    text_rows = text_keys.shape[0]
    rows_kept = (TS - TS // 4) * TS * TS
    bf16, f32 = jnp.bfloat16, jnp.float32
    dma = pltpu.SemaphoreType.DMA
    hbm = pl.BlockSpec(memory_space=pl.ANY)
    keys_seen = 3 * rows_kept + count * text_rows
    return pl.pallas_call(
        functools.partial(row_kernel, count, rows_kept, head_count, text_rows),
        out_shape=jax.ShapeDtypeStruct(queries.shape, bf16),
        in_specs=[hbm] * 5 + [pl.BlockSpec(memory_space=pltpu.SMEM)],
        out_specs=hbm,
        scratch_shapes=[
            pltpu.VMEM((tokens, width), bf16),
            pltpu.VMEM((rows_kept, width), bf16),
            pltpu.VMEM((rows_kept, width), bf16),
            pltpu.VMEM(text_keys.shape, bf16),
            pltpu.VMEM(text_keys.shape, bf16),
            pltpu.VMEM((HEAD_GROUPS, text_rows, 2 * width + HEAD_DIM), bf16),
            pltpu.VMEM((count * text_rows, 2 * width + HEAD_DIM), bf16),
            pltpu.VMEM((2, rows_kept, width), bf16),
            pltpu.VMEM((2, rows_kept, width), bf16),
            pltpu.VMEM((tokens, width), bf16),
            pltpu.VMEM((head_count, tokens, HEAD_DIM), f32),
            pltpu.VMEM((head_count, tokens, HEAD_DIM), f32),
            pltpu.VMEM((head_count, tokens, HEAD_DIM), f32),
            dma((5,)),
            dma((head_count,)),
            dma((count,)),
            dma((count,)),
            dma((2, head_count, 2)),
            dma((2, head_count, 2)),
        ],
        compiler_params=pltpu.CompilerParams(
            collective_id=0, has_side_effects=True, vmem_limit_bytes=48 * 1024 * 1024
        ),
        cost_estimate=pl.CostEstimate(
            flops=4 * tokens * keys_seen * width,
            bytes_accessed=10 * tokens * width,
            transcendentals=tokens * keys_seen * head_count,
        ),
    )(queries, keys, values, text_keys, text_values, text_mask)


def solution(mesh):
    tiles = mesh.shape["tile"] // HEAD_GROUPS

    def shards(*blocks):
        one_row = tiles <= 4 and blocks[3].shape[0] % 16 == 0
        return (row_shards if one_row else gathered_shards)(*blocks)

    return jax.shard_map(
        shards,
        mesh=mesh,
        in_specs=(
            P(("req", "tile"), None, None),
            P(("req", "tile"), None, None),
            P(("req", "tile"), None, None),
            P(("req", "tile"), None),
            P(("req", "tile"), None),
            P(("req", "tile")),
        ),
        out_specs=P(("req", "tile"), None, None),
        check_vma=False,
    )
```

```python
import functools
import math

import jax
import jax.numpy as jnp
from jax import lax
from jax.experimental import pallas as pl
from jax.experimental.pallas import tpu as pltpu
from jax.sharding import PartitionSpec as P

MESH = pl.DeviceIdType.MESH
EXP2_SCALE = math.log2(math.e) / math.sqrt(128)

TS = 8
HEAD_DIM = 128
HEAD_GROUPS = 4


MASKED = -1e30


def passed_along(value, axis, steps):
    count = lax.axis_size(axis)
    first, last = (max(0, -steps), min(count, count - steps))
    return lax.ppermute(value, axis, [(source, source + steps) for source in range(first, last)])


def shortened(value):
    return jax.tree.map(lambda a: a.astype(jnp.bfloat16) if a.dtype == jnp.float32 else a, value)


def fold_block(running, query_heads, key_block, value_block, key_keep):
    row_top, row_total, summed = running
    head_count = query_heads.shape[1]
    key_heads = key_block.reshape(key_block.shape[0], head_count, HEAD_DIM)
    value_heads = value_block.reshape(value_block.shape[0], head_count, HEAD_DIM)
    scores = jnp.einsum("qhd,khd->hqk", query_heads, key_heads, preferred_element_type=jnp.float32)
    scores = scores * (1.0 / math.sqrt(HEAD_DIM))
    scores = jnp.where(key_keep[None, None, :], scores, MASKED)
    new_top = jnp.maximum(row_top, jnp.max(scores, axis=-1))
    scale_down = jnp.exp(row_top - new_top)
    exp_terms = jnp.where(key_keep[None, None, :], jnp.exp(scores - new_top[:, :, None]), 0.0)
    row_total = row_total * scale_down + jnp.sum(exp_terms, axis=-1)
    weights = exp_terms.astype(jnp.bfloat16)
    summed = summed * scale_down[:, :, None] + jnp.einsum(
        "hqk,khd->hqd", weights, value_heads, preferred_element_type=jnp.float32
    )
    return (new_top, row_total, summed)


def gathered_shards(queries, keys, values, text_keys, text_values, text_mask):
    tokens = queries.shape[1]
    lane_width = queries.shape[2]
    head_count = lane_width // HEAD_DIM
    query_heads = queries[0].reshape(tokens, head_count, HEAD_DIM)
    own_pair = jnp.stack([keys[0], values[0]])
    group_count = HEAD_GROUPS
    tiles_all = lax.axis_size("tile") // group_count
    grid_w = min(4, tiles_all)
    grid_h = min(4, tiles_all // grid_w)
    grid_f = tiles_all // (grid_w * grid_h)
    frames_valid = grid_f * TS - TS // 4
    my_index = lax.axis_index("tile")
    tile_id = my_index // group_count
    head_group = my_index % group_count
    w_pos = tile_id % grid_w
    h_pos = tile_id // grid_w % grid_h
    f_pos = tile_id // (grid_w * grid_h)
    local_frame = jnp.arange(tokens, dtype=jnp.int32) // (TS * TS)

    def keep_mask(off_frame, off_height, off_width):
        inside = (
            (f_pos + off_frame >= 0)
            & (f_pos + off_frame < grid_f)
            & (h_pos + off_height >= 0)
            & (h_pos + off_height < grid_h)
            & (w_pos + off_width >= 0)
            & (w_pos + off_width < grid_w)
        )
        return inside & ((f_pos + off_frame) * TS + local_frame < frames_valid)

    running = (
        jnp.full((head_count, tokens), MASKED, jnp.float32),
        jnp.zeros((head_count, tokens), jnp.float32),
        jnp.zeros((head_count, tokens, HEAD_DIM), jnp.float32),
    )
    text_flags = text_mask.astype(jnp.bfloat16)
    piece_keys = lax.dynamic_slice_in_dim(
        lax.all_gather(text_keys, "tile", axis=0, tiled=True),
        head_group * lane_width,
        lane_width,
        1,
    )
    piece_values = lax.dynamic_slice_in_dim(
        lax.all_gather(text_values, "tile", axis=0, tiled=True),
        head_group * lane_width,
        lane_width,
        1,
    )
    running = fold_block(
        running,
        query_heads,
        piece_keys,
        piece_values,
        lax.all_gather(text_flags, "tile", axis=0, tiled=True) > 0.5,
    )
    running = fold_block(running, query_heads, own_pair[0], own_pair[1], keep_mask(0, 0, 0))
    width_set = {0: own_pair}
    for off_width in (-1, 1):
        width_set[off_width] = passed_along(own_pair, "tile", -off_width * group_count)
    width_offsets = sorted(width_set)
    row_stack = jnp.stack([width_set[spot] for spot in width_offsets])
    height_set = {0: row_stack}
    if grid_h > 1:
        for off_height in (-1, 1):
            height_set[off_height] = passed_along(
                shortened(row_stack), "tile", -off_height * grid_w * group_count
            ).astype(row_stack.dtype)
    height_offsets = sorted(height_set)
    slab_stack = jnp.stack([height_set[spot] for spot in height_offsets])

    def fold_slab(state_now, slab_pairs, off_frame):
        for h_slot, off_height in enumerate(height_offsets):
            for w_slot, off_width in enumerate(width_offsets):
                if off_frame == 0 and off_height == 0 and (off_width == 0):
                    continue
                state_now = fold_block(
                    state_now,
                    query_heads,
                    slab_pairs[h_slot, w_slot, 0],
                    slab_pairs[h_slot, w_slot, 1],
                    keep_mask(off_frame, off_height, off_width),
                )
        return state_now

    running = fold_slab(running, slab_stack, 0)
    if grid_f > 1:
        for off_frame in (-1, 1):
            got_slab = passed_along(
                shortened(slab_stack), "tile", -off_frame * grid_h * grid_w * group_count
            ).astype(slab_stack.dtype)
            running = fold_slab(running, got_slab, off_frame)
    row_top, row_total, summed = running
    result = summed / row_total[:, :, None]
    result = jnp.transpose(result, (1, 0, 2)).reshape(tokens, lane_width)
    return result.astype(jnp.bfloat16)[None]


def row_kernel(
    count, rows_kept, head_count, text_rows,
    q_hbm, k_hbm, v_hbm, tk_hbm, tv_hbm, mask_hbm, out_hbm,
    q_ref, k_ref, v_ref, tk_ref, tv_ref, mask_ref, packets, flags_in, text, near_k, near_v, out_ref,
    top_ref, total_ref, summed_ref,
    in_sem, out_sem, plane_send, plane_recv, chain_send, chain_recv, near_send, near_recv,
):
    groups = HEAD_GROUPS
    tiles = count // groups
    per_source = 2 * head_count
    flag_at = groups * per_source
    me = lax.axis_index("tile")
    tile = me // groups
    group = lax.rem(me, groups)
    first_here = tile * groups
    has_left = tile > 0
    has_right = tile < tiles - 1
    target = (me + groups, me - groups)
    sends = (has_right, has_left)
    receives = (has_left, has_right)

    def partner(step):
        return first_here + lax.rem(group + step, groups)

    barrier = pltpu.get_barrier_semaphore()
    for step in range(1, groups):
        pl.semaphore_signal(barrier, inc=1, device_id={"tile": partner(step)}, device_id_type=MESH)
    for side in range(2):

        @pl.when(sends[side])
        def _():
            pl.semaphore_signal(barrier, inc=1, device_id={"tile": target[side]}, device_id_type=MESH)

    loads = [
        pltpu.make_async_copy(mask_hbm, mask_ref, in_sem.at[0]),
        pltpu.make_async_copy(tk_hbm, tk_ref, in_sem.at[1]),
        pltpu.make_async_copy(tv_hbm, tv_ref, in_sem.at[2]),
        pltpu.make_async_copy(q_hbm.at[0], q_ref, in_sem.at[3]),
        pltpu.make_async_copy(k_hbm.at[0, pl.ds(0, rows_kept), :], k_ref, in_sem.at[4]),
        pltpu.make_async_copy(v_hbm.at[0, pl.ds(0, rows_kept), :], v_ref, in_sem.at[5]),
    ]
    for load in loads:
        load.start()

    def near_copy(side, head, which):
        cols = pl.ds(head * HEAD_DIM, HEAD_DIM)
        source, landing = ((k_hbm, near_k), (v_hbm, near_v))[which]
        return pltpu.make_async_remote_copy(
            src_ref=source.at[0, pl.ds(0, rows_kept), cols],
            dst_ref=landing.at[side, :, cols],
            send_sem=near_send.at[side, head, which],
            recv_sem=near_recv.at[side, head, which],
            device_id={"tile": target[side]},
            device_id_type=MESH,
        )

    def start_near(head, which):
        for side in range(2):

            @pl.when(sends[side])
            def _():
                near_copy(side, head, which).start()

    def plane_copies(step):
        to = partner(step)
        made = []
        for which, (source, landing) in enumerate(
            (
                (packets.at[lax.rem(group + step, groups)], text.at[tile, pl.ds(group * per_source, per_source)]),
                (flags_in.at[group], flags_in.at[group]),
            )
        ):
            made.append(
                pltpu.make_async_remote_copy(
                    src_ref=source,
                    dst_ref=landing,
                    send_sem=plane_send.at[step, which],
                    recv_sem=plane_recv.at[step, which],
                    device_id={"tile": to},
                    device_id_type=MESH,
                )
            )
        return made

    def chain_copy(side, hop, owner):
        return pltpu.make_async_remote_copy(
            src_ref=text.at[owner],
            dst_ref=text.at[owner],
            send_sem=chain_send.at[side, hop],
            recv_sem=chain_recv.at[side, hop],
            device_id={"tile": target[side]},
            device_id_type=MESH,
        )

    def chain_sent(side, hop):
        owner = tile - hop if side == 0 else tile + hop
        there = owner >= 0 if side == 0 else owner < tiles
        return owner, there & sends[side]

    def chain_got(side, hop):
        owner = tile - hop - 1 if side == 0 else tile + hop + 1
        return owner, owner >= 0 if side == 0 else owner < tiles

    def start_chain(hop):
        for side in range(2):
            owner, there = chain_sent(side, hop)

            @pl.when(there)
            def _():
                chain_copy(side, hop, owner).start()

    def wait_chain(hop):
        for side in range(2):
            owner, there = chain_got(side, hop)

            @pl.when(there)
            def _():
                chain_copy(side, hop, owner).wait_recv()

    def fold(head, keys, values, keep, first):
        query = q_ref[:, head * HEAD_DIM : (head + 1) * HEAD_DIM]
        scores = lax.dot_general(query, keys, (((1,), (1,)), ((), ())), preferred_element_type=jnp.float32)
        if keep is not None:
            scores = jnp.where(keep, scores, MASKED)
        block_top = jnp.broadcast_to(jnp.max(scores, axis=1, keepdims=True), (scores.shape[0], HEAD_DIM))
        new_top = block_top if first else jnp.maximum(top_ref[head], block_top)
        pieces = [
            jnp.exp2((scores[:, at : at + HEAD_DIM] - new_top) * EXP2_SCALE) for at in range(0, keys.shape[0], HEAD_DIM)
        ]
        part = functools.reduce(lambda a, b: a + b, pieces)
        weights = jnp.concatenate([piece.astype(jnp.bfloat16) for piece in pieces], axis=1)
        product = jnp.dot(weights, values, preferred_element_type=jnp.float32)
        if first:
            total_ref[head] = part
            summed_ref[head] = product
        else:
            scale_down = jnp.exp2((top_ref[head] - new_top) * EXP2_SCALE)
            total_ref[head] = total_ref[head] * scale_down + part
            summed_ref[head] = summed_ref[head] * scale_down + product
        top_ref[head] = new_top

    def fold_near(head):
        cols = slice(head * HEAD_DIM, (head + 1) * HEAD_DIM)
        for side in range(2):

            @pl.when(receives[side])
            def _():
                for which in range(2):
                    near_copy(side, head, which).wait_recv()
                fold(head, near_k[side, :, cols], near_v[side, :, cols], None, False)

    def out_copy(head):
        cols = pl.ds(head * HEAD_DIM, HEAD_DIM)
        return pltpu.make_async_copy(out_ref.at[:, cols], out_hbm.at[0, :, cols], out_sem.at[head])

    loads[0].wait()
    row_of = lax.broadcasted_iota(jnp.int32, (text_rows, HEAD_DIM), 0)
    lane_of = lax.broadcasted_iota(jnp.int32, (text_rows, HEAD_DIM), 1)
    flags = jnp.zeros((text_rows, HEAD_DIM), jnp.float32)
    for row in range(text_rows):
        flags = jnp.where((row_of == row) & (lane_of == me), mask_ref[row].astype(jnp.float32), flags)
    flags_in[group] = flags.astype(jnp.bfloat16)
    loads[1].wait()
    loads[2].wait()
    for to in range(groups):
        for which, source in enumerate((tk_ref, tv_ref)):
            for head in range(head_count):
                at = (to * head_count + head) * HEAD_DIM
                packets[to, which * head_count + head] = source[:, at : at + HEAD_DIM]
    text[tile, pl.ds(group * per_source, per_source)] = packets[group]

    pl.semaphore_wait(barrier, groups - 1 + has_left.astype(jnp.int32) + has_right.astype(jnp.int32))

    for step in range(1, groups):
        for copy in plane_copies(step):
            copy.start()
    start_near(0, 0)
    start_near(0, 1)
    for step in range(1, groups):
        for copy in plane_copies(step):
            copy.wait_recv()
    text[tile, flag_at] = functools.reduce(lambda a, b: a + b, [flags_in[source] for source in range(groups)])
    start_chain(0)
    start_near(1, 0)

    for load in loads[3:]:
        load.wait()
    for head in range(head_count):
        cols = slice(head * HEAD_DIM, (head + 1) * HEAD_DIM)
        fold(head, k_ref[:, cols], v_ref[:, cols], None, True)

    rest = [(1, 1)] + [(head, which) for head in range(2, head_count) for which in range(2)]
    folded = 0
    for hop in range(1, tiles - 1):
        wait_chain(hop - 1)
        start_chain(hop)
        if rest:
            start_near(*rest.pop(0))
        if hop == tiles - 2:
            for item in rest:
                start_near(*item)
        if folded < head_count - 1:
            fold_near(folded)
            folded += 1
    wait_chain(tiles - 2)

    wide_row = lax.broadcasted_iota(jnp.int32, (count * text_rows, HEAD_DIM), 0)
    wide_lane = lax.broadcasted_iota(jnp.int32, (count * text_rows, HEAD_DIM), 1)
    spread = jnp.concatenate([text[source // groups, flag_at] for source in range(count)], axis=0)
    spread = jnp.where(wide_lane == wide_row // text_rows, spread, jnp.zeros_like(spread))
    keep_row = lax.dot_general(
        jnp.ones((8, HEAD_DIM), jnp.bfloat16), spread, (((1,), (1,)), ((), ())), preferred_element_type=jnp.float32
    )[0:1, :]
    keep = jnp.broadcast_to(keep_row, (q_ref.shape[0], keep_row.shape[1])) > 0.5

    def text_piece(at):
        return jnp.concatenate(
            [text[source // groups, source % groups * per_source + at] for source in range(count)], axis=0
        )

    for head in range(head_count):
        fold(head, text_piece(head), text_piece(head_count + head), keep, False)

    for head in range(head_count):
        if head >= folded:
            fold_near(head)
        cols = slice(head * HEAD_DIM, (head + 1) * HEAD_DIM)
        total = jnp.sum(total_ref[head], axis=1, keepdims=True)
        out_ref[:, cols] = (summed_ref[head] / total).astype(out_ref.dtype)
        out_copy(head).start()

    for step in range(1, groups):
        for copy in plane_copies(step):
            copy.wait_send()
    for side in range(2):

        @pl.when(sends[side])
        def _():
            for head in range(head_count):
                for which in range(2):
                    near_copy(side, head, which).wait_send()

        for hop in range(tiles - 1):
            owner, there = chain_sent(side, hop)

            @pl.when(there)
            def _():
                chain_copy(side, hop, owner).wait_send()

    for head in range(head_count):
        out_copy(head).wait()


def row_shards(queries, keys, values, text_keys, text_values, text_mask):
    tokens, width = queries.shape[1:]
    head_count = width // HEAD_DIM
    count = lax.axis_size("tile")
    tiles = count // HEAD_GROUPS
    text_rows = text_keys.shape[0]
    rows_kept = (TS - TS // 4) * TS * TS
    bf16, f32 = jnp.bfloat16, jnp.float32
    dma = pltpu.SemaphoreType.DMA
    hbm = pl.BlockSpec(memory_space=pltpu.HBM)
    keys_seen = 3 * rows_kept + count * text_rows
    per_source = 2 * head_count
    return pl.pallas_call(
        functools.partial(row_kernel, count, rows_kept, head_count, text_rows),
        out_shape=jax.ShapeDtypeStruct(queries.shape, bf16),
        in_specs=[hbm] * 6,
        out_specs=hbm,
        scratch_shapes=[
            pltpu.VMEM((tokens, width), bf16),
            pltpu.VMEM((rows_kept, width), bf16),
            pltpu.VMEM((rows_kept, width), bf16),
            pltpu.VMEM(text_keys.shape, bf16),
            pltpu.VMEM(text_keys.shape, bf16),
            pltpu.SMEM((text_rows,), jnp.int32),
            pltpu.VMEM((HEAD_GROUPS, per_source, text_rows, HEAD_DIM), bf16),
            pltpu.VMEM((HEAD_GROUPS, text_rows, HEAD_DIM), bf16),
            pltpu.VMEM((tiles, HEAD_GROUPS * per_source + 1, text_rows, HEAD_DIM), bf16),
            pltpu.VMEM((2, rows_kept, width), bf16),
            pltpu.VMEM((2, rows_kept, width), bf16),
            pltpu.VMEM((tokens, width), bf16),
            pltpu.VMEM((head_count, tokens, HEAD_DIM), f32),
            pltpu.VMEM((head_count, tokens, HEAD_DIM), f32),
            pltpu.VMEM((head_count, tokens, HEAD_DIM), f32),
            dma((6,)),
            dma((head_count,)),
            dma((HEAD_GROUPS, 2)),
            dma((HEAD_GROUPS, 2)),
            dma((2, tiles - 1)),
            dma((2, tiles - 1)),
            dma((2, head_count, 2)),
            dma((2, head_count, 2)),
        ],
        compiler_params=pltpu.CompilerParams(
            collective_id=0, has_side_effects=True, vmem_limit_bytes=56 * 1024 * 1024
        ),
        cost_estimate=pl.CostEstimate(
            flops=4 * tokens * keys_seen * width,
            bytes_accessed=10 * tokens * width,
            transcendentals=tokens * keys_seen * head_count,
        ),
    )(queries, keys, values, text_keys, text_values, text_mask)


def solution(mesh):
    tiles = mesh.shape["tile"] // HEAD_GROUPS

    def shards(*blocks):
        one_row = 1 < tiles <= 4 and blocks[3].shape[0] % 16 == 0
        return (row_shards if one_row else gathered_shards)(*blocks)

    return jax.shard_map(
        shards,
        mesh=mesh,
        in_specs=(
            P(("req", "tile"), None, None),
            P(("req", "tile"), None, None),
            P(("req", "tile"), None, None),
            P(("req", "tile"), None),
            P(("req", "tile"), None),
            P(("req", "tile")),
        ),
        out_specs=P(("req", "tile"), None, None),
        check_vma=False,
    )
```

```python
import functools
import math

import jax
import jax.numpy as jnp
from jax import lax
from jax.experimental import pallas as pl
from jax.experimental.pallas import tpu as pltpu
from jax.sharding import PartitionSpec as P

MESH = pl.DeviceIdType.MESH
EXP2_SCALE = math.log2(math.e) / math.sqrt(128)

TS = 8
HEAD_DIM = 128
HEAD_GROUPS = 4


MASKED = -1e30


def passed_along(value, axis, steps):
    count = lax.axis_size(axis)
    first, last = (max(0, -steps), min(count, count - steps))
    return lax.ppermute(value, axis, [(source, source + steps) for source in range(first, last)])


def shortened(value):
    return jax.tree.map(lambda a: a.astype(jnp.bfloat16) if a.dtype == jnp.float32 else a, value)


def fold_block(running, query_heads, key_block, value_block, key_keep):
    row_top, row_total, summed = running
    head_count = query_heads.shape[1]
    key_heads = key_block.reshape(key_block.shape[0], head_count, HEAD_DIM)
    value_heads = value_block.reshape(value_block.shape[0], head_count, HEAD_DIM)
    scores = jnp.einsum("qhd,khd->hqk", query_heads, key_heads, preferred_element_type=jnp.float32)
    scores = scores * (1.0 / math.sqrt(HEAD_DIM))
    scores = jnp.where(key_keep[None, None, :], scores, MASKED)
    new_top = jnp.maximum(row_top, jnp.max(scores, axis=-1))
    scale_down = jnp.exp(row_top - new_top)
    exp_terms = jnp.where(key_keep[None, None, :], jnp.exp(scores - new_top[:, :, None]), 0.0)
    row_total = row_total * scale_down + jnp.sum(exp_terms, axis=-1)
    weights = exp_terms.astype(jnp.bfloat16)
    summed = summed * scale_down[:, :, None] + jnp.einsum(
        "hqk,khd->hqd", weights, value_heads, preferred_element_type=jnp.float32
    )
    return (new_top, row_total, summed)


def gathered_shards(queries, keys, values, text_keys, text_values, text_mask):
    tokens = queries.shape[1]
    lane_width = queries.shape[2]
    head_count = lane_width // HEAD_DIM
    query_heads = queries[0].reshape(tokens, head_count, HEAD_DIM)
    own_pair = jnp.stack([keys[0], values[0]])
    group_count = HEAD_GROUPS
    tiles_all = lax.axis_size("tile") // group_count
    grid_w = min(4, tiles_all)
    grid_h = min(4, tiles_all // grid_w)
    grid_f = tiles_all // (grid_w * grid_h)
    frames_valid = grid_f * TS - TS // 4
    my_index = lax.axis_index("tile")
    tile_id = my_index // group_count
    head_group = my_index % group_count
    w_pos = tile_id % grid_w
    h_pos = tile_id // grid_w % grid_h
    f_pos = tile_id // (grid_w * grid_h)
    local_frame = jnp.arange(tokens, dtype=jnp.int32) // (TS * TS)

    def keep_mask(off_frame, off_height, off_width):
        inside = (
            (f_pos + off_frame >= 0)
            & (f_pos + off_frame < grid_f)
            & (h_pos + off_height >= 0)
            & (h_pos + off_height < grid_h)
            & (w_pos + off_width >= 0)
            & (w_pos + off_width < grid_w)
        )
        return inside & ((f_pos + off_frame) * TS + local_frame < frames_valid)

    running = (
        jnp.full((head_count, tokens), MASKED, jnp.float32),
        jnp.zeros((head_count, tokens), jnp.float32),
        jnp.zeros((head_count, tokens, HEAD_DIM), jnp.float32),
    )
    text_flags = text_mask.astype(jnp.bfloat16)
    piece_keys = lax.dynamic_slice_in_dim(
        lax.all_gather(text_keys, "tile", axis=0, tiled=True),
        head_group * lane_width,
        lane_width,
        1,
    )
    piece_values = lax.dynamic_slice_in_dim(
        lax.all_gather(text_values, "tile", axis=0, tiled=True),
        head_group * lane_width,
        lane_width,
        1,
    )
    running = fold_block(
        running,
        query_heads,
        piece_keys,
        piece_values,
        lax.all_gather(text_flags, "tile", axis=0, tiled=True) > 0.5,
    )
    running = fold_block(running, query_heads, own_pair[0], own_pair[1], keep_mask(0, 0, 0))
    width_set = {0: own_pair}
    for off_width in (-1, 1):
        width_set[off_width] = passed_along(own_pair, "tile", -off_width * group_count)
    width_offsets = sorted(width_set)
    row_stack = jnp.stack([width_set[spot] for spot in width_offsets])
    height_set = {0: row_stack}
    if grid_h > 1:
        for off_height in (-1, 1):
            height_set[off_height] = passed_along(
                shortened(row_stack), "tile", -off_height * grid_w * group_count
            ).astype(row_stack.dtype)
    height_offsets = sorted(height_set)
    slab_stack = jnp.stack([height_set[spot] for spot in height_offsets])

    def fold_slab(state_now, slab_pairs, off_frame):
        for h_slot, off_height in enumerate(height_offsets):
            for w_slot, off_width in enumerate(width_offsets):
                if off_frame == 0 and off_height == 0 and (off_width == 0):
                    continue
                state_now = fold_block(
                    state_now,
                    query_heads,
                    slab_pairs[h_slot, w_slot, 0],
                    slab_pairs[h_slot, w_slot, 1],
                    keep_mask(off_frame, off_height, off_width),
                )
        return state_now

    running = fold_slab(running, slab_stack, 0)
    if grid_f > 1:
        for off_frame in (-1, 1):
            got_slab = passed_along(
                shortened(slab_stack), "tile", -off_frame * grid_h * grid_w * group_count
            ).astype(slab_stack.dtype)
            running = fold_slab(running, got_slab, off_frame)
    row_top, row_total, summed = running
    result = summed / row_total[:, :, None]
    result = jnp.transpose(result, (1, 0, 2)).reshape(tokens, lane_width)
    return result.astype(jnp.bfloat16)[None]


def row_kernel(
    count, rows_kept, head_count, text_rows,
    q_hbm, k_hbm, v_hbm, tk_hbm, tv_hbm, mask_hbm, out_ref,
    q_ref, k_ref, v_ref, tk_ref, tv_ref, mask_ref, packets, flags_in, text, near_k, near_v,
    top_ref, total_ref, summed_ref, held_weights, held_top,
    in_sem, plane_send, plane_recv, chain_send, chain_recv, near_send, near_recv,
):
    groups = HEAD_GROUPS
    tiles = count // groups
    per_source = 2 * head_count
    flag_at = groups * per_source
    me = lax.axis_index("tile")
    tile = me // groups
    group = lax.rem(me, groups)
    first_here = tile * groups
    has_left = tile > 0
    has_right = tile < tiles - 1
    target = (me + groups, me - groups)
    sends = (has_right, has_left)
    receives = (has_left, has_right)

    def partner(step):
        return first_here + lax.rem(group + step, groups)

    barrier = pltpu.get_barrier_semaphore()
    for step in range(1, groups):
        pl.semaphore_signal(barrier, inc=1, device_id={"tile": partner(step)}, device_id_type=MESH)
    for side in range(2):

        @pl.when(sends[side])
        def _():
            pl.semaphore_signal(barrier, inc=1, device_id={"tile": target[side]}, device_id_type=MESH)

    loads = [
        pltpu.make_async_copy(mask_hbm, mask_ref, in_sem.at[0]),
        pltpu.make_async_copy(tk_hbm, tk_ref, in_sem.at[1]),
        pltpu.make_async_copy(tv_hbm, tv_ref, in_sem.at[2]),
        pltpu.make_async_copy(q_hbm.at[0], q_ref, in_sem.at[3]),
        pltpu.make_async_copy(k_hbm.at[0, pl.ds(0, rows_kept), :], k_ref, in_sem.at[4]),
        pltpu.make_async_copy(v_hbm.at[0, pl.ds(0, rows_kept), :], v_ref, in_sem.at[5]),
    ]
    for load in loads:
        load.start()

    def near_copy(side, head, which):
        cols = pl.ds(head * HEAD_DIM, HEAD_DIM)
        source, landing = ((k_hbm, near_k), (v_hbm, near_v))[which]
        return pltpu.make_async_remote_copy(
            src_ref=source.at[0, pl.ds(0, rows_kept), cols],
            dst_ref=landing.at[side, :, cols],
            send_sem=near_send.at[side, head, which],
            recv_sem=near_recv.at[side, head, which],
            device_id={"tile": target[side]},
            device_id_type=MESH,
        )

    def start_near(head, which):
        for side in range(2):

            @pl.when(sends[side])
            def _():
                near_copy(side, head, which).start()

    def plane_copies(step):
        to = partner(step)
        made = []
        for which, (source, landing) in enumerate(
            (
                (packets.at[lax.rem(group + step, groups)], text.at[tile, pl.ds(group * per_source, per_source)]),
                (flags_in.at[group], flags_in.at[group]),
            )
        ):
            made.append(
                pltpu.make_async_remote_copy(
                    src_ref=source,
                    dst_ref=landing,
                    send_sem=plane_send.at[step, which],
                    recv_sem=plane_recv.at[step, which],
                    device_id={"tile": to},
                    device_id_type=MESH,
                )
            )
        return made

    def chain_copy(side, hop, owner):
        return pltpu.make_async_remote_copy(
            src_ref=text.at[owner],
            dst_ref=text.at[owner],
            send_sem=chain_send.at[side, hop],
            recv_sem=chain_recv.at[side, hop],
            device_id={"tile": target[side]},
            device_id_type=MESH,
        )

    def chain_sent(side, hop):
        owner = tile - hop if side == 0 else tile + hop
        there = owner >= 0 if side == 0 else owner < tiles
        return owner, there & sends[side]

    def chain_got(side, hop):
        owner = tile - hop - 1 if side == 0 else tile + hop + 1
        return owner, owner >= 0 if side == 0 else owner < tiles

    def start_chain(hop):
        for side in range(2):
            owner, there = chain_sent(side, hop)

            @pl.when(there)
            def _():
                chain_copy(side, hop, owner).start()

    def wait_chain(hop):
        for side in range(2):
            owner, there = chain_got(side, hop)

            @pl.when(there)
            def _():
                chain_copy(side, hop, owner).wait_recv()

    def weigh(head, keys, keep, first):
        query = q_ref[:, head * HEAD_DIM : (head + 1) * HEAD_DIM]
        scores = lax.dot_general(query, keys, (((1,), (1,)), ((), ())), preferred_element_type=jnp.float32)
        if keep is not None:
            scores = jnp.where(keep, scores, MASKED)
        block_top = jnp.broadcast_to(jnp.max(scores, axis=1, keepdims=True), (scores.shape[0], HEAD_DIM))
        new_top = block_top if first else jnp.maximum(top_ref[head], block_top)
        pieces = [
            jnp.exp2((scores[:, at : at + HEAD_DIM] - new_top) * EXP2_SCALE) for at in range(0, keys.shape[0], HEAD_DIM)
        ]
        part = functools.reduce(lambda a, b: a + b, pieces)
        weights = jnp.concatenate([piece.astype(jnp.bfloat16) for piece in pieces], axis=1)
        if first:
            total_ref[head] = part
            summed = None
        else:
            scale_down = jnp.exp2((top_ref[head] - new_top) * EXP2_SCALE)
            total_ref[head] = total_ref[head] * scale_down + part
            summed = summed_ref[head] * scale_down
        top_ref[head] = new_top
        return weights, summed

    def fold(head, keys, values, keep, first):
        weights, summed = weigh(head, keys, keep, first)
        product = jnp.dot(weights, values, preferred_element_type=jnp.float32)
        summed_ref[head] = product if summed is None else summed + product

    def head_cols(head):
        return slice(head * HEAD_DIM, (head + 1) * HEAD_DIM)

    def fold_near(head):
        cols = head_cols(head)
        for side in range(2):

            @pl.when(receives[side])
            def _():
                for which in range(2):
                    near_copy(side, head, which).wait_recv()
                fold(head, near_k[side, :, cols], near_v[side, :, cols], None, False)

    def weigh_near(head):
        for side in range(2):

            @pl.when(receives[side])
            def _():
                near_copy(side, head, 0).wait_recv()
                weights, summed = weigh(head, near_k[side, :, head_cols(head)], None, False)
                summed_ref[head] = summed
                held_weights[side] = weights
                held_top[side] = top_ref[head]

    def apply_near(head):
        for side in range(2):

            @pl.when(receives[side])
            def _():
                near_copy(side, head, 1).wait_recv()
                product = jnp.dot(
                    held_weights[side], near_v[side, :, head_cols(head)], preferred_element_type=jnp.float32
                )
                since = jnp.exp2((held_top[side] - top_ref[head]) * EXP2_SCALE)
                summed_ref[head] = summed_ref[head] + product * since

    def finish(head):
        total = jnp.sum(total_ref[head], axis=1, keepdims=True)
        out_ref[0, :, head_cols(head)] = (summed_ref[head] / total).astype(out_ref.dtype)

    def fold_own(head):
        fold(head, k_ref[:, head_cols(head)], v_ref[:, head_cols(head)], None, True)

    pl.semaphore_wait(barrier, groups - 1 + has_left.astype(jnp.int32) + has_right.astype(jnp.int32))
    waiting = [(head, which) for head in range(head_count) for which in range(2)]
    for item in waiting[:2]:
        start_near(*item)

    loads[0].wait()
    row_of = lax.broadcasted_iota(jnp.int32, (text_rows, HEAD_DIM), 0)
    lane_of = lax.broadcasted_iota(jnp.int32, (text_rows, HEAD_DIM), 1)
    flags = jnp.zeros((text_rows, HEAD_DIM), jnp.float32)
    for row in range(text_rows):
        flags = jnp.where((row_of == row) & (lane_of == me), mask_ref[row].astype(jnp.float32), flags)
    flags_in[group] = flags.astype(jnp.bfloat16)
    loads[1].wait()
    loads[2].wait()
    for to in range(groups):
        for which, source in enumerate((tk_ref, tv_ref)):
            for head in range(head_count):
                at = (to * head_count + head) * HEAD_DIM
                packets[to, which * head_count + head] = source[:, at : at + HEAD_DIM]
    text[tile, pl.ds(group * per_source, per_source)] = packets[group]
    for step in range(1, groups):
        for copy in plane_copies(step):
            copy.start()
    for load in loads[3:]:
        load.wait()
    fold_own(0)
    for step in range(1, groups):
        for copy in plane_copies(step):
            copy.wait_recv()
    text[tile, flag_at] = functools.reduce(lambda a, b: a + b, [flags_in[source] for source in range(groups)])

    start_chain(0)
    for item in waiting[2:4] if tiles > 2 else waiting[2:]:
        start_near(*item)
    for head in range(1, head_count):
        fold_own(head)
    folded = 0
    for hop in range(1, tiles - 1):
        if folded < min(2, head_count - 1):
            fold_near(folded)
            folded += 1
        wait_chain(hop - 1)
        start_chain(hop)
        for item in waiting[3 + hop : 4 + hop] if hop < tiles - 2 else waiting[3 + hop :]:
            start_near(*item)
    for head in range(folded, head_count - 1):
        fold_near(head)
    weigh_near(head_count - 1)
    wait_chain(tiles - 2)

    wide_row = lax.broadcasted_iota(jnp.int32, (count * text_rows, HEAD_DIM), 0)
    wide_lane = lax.broadcasted_iota(jnp.int32, (count * text_rows, HEAD_DIM), 1)
    spread = jnp.concatenate([text[source // groups, flag_at] for source in range(count)], axis=0)
    spread = jnp.where(wide_lane == wide_row // text_rows, spread, jnp.zeros_like(spread))
    keep_row = lax.dot_general(
        jnp.ones((8, HEAD_DIM), jnp.bfloat16), spread, (((1,), (1,)), ((), ())), preferred_element_type=jnp.float32
    )[0:1, :]
    keep = jnp.broadcast_to(keep_row, (q_ref.shape[0], keep_row.shape[1])) > 0.5

    def text_piece(at):
        return jnp.concatenate(
            [text[source // groups, source % groups * per_source + at] for source in range(count)], axis=0
        )

    for head in range(head_count):
        fold(head, text_piece(head), text_piece(head_count + head), keep, False)
        if head == head_count - 1:
            apply_near(head)
        finish(head)

    for step in range(1, groups):
        for copy in plane_copies(step):
            copy.wait_send()
    for side in range(2):

        @pl.when(sends[side])
        def _():
            for head in range(head_count):
                for which in range(2):
                    near_copy(side, head, which).wait_send()

        for hop in range(tiles - 1):
            owner, there = chain_sent(side, hop)

            @pl.when(there)
            def _():
                chain_copy(side, hop, owner).wait_send()


def row_shards(queries, keys, values, text_keys, text_values, text_mask):
    tokens, width = queries.shape[1:]
    head_count = width // HEAD_DIM
    count = lax.axis_size("tile")
    tiles = count // HEAD_GROUPS
    text_rows = text_keys.shape[0]
    rows_kept = (TS - TS // 4) * TS * TS
    bf16, f32 = jnp.bfloat16, jnp.float32
    dma = pltpu.SemaphoreType.DMA
    hbm = pl.BlockSpec(memory_space=pltpu.HBM)
    keys_seen = 3 * rows_kept + count * text_rows
    per_source = 2 * head_count
    return pl.pallas_call(
        functools.partial(row_kernel, count, rows_kept, head_count, text_rows),
        out_shape=pltpu.VMEM(queries.shape, bf16),
        in_specs=[hbm] * 6,
        out_specs=pl.BlockSpec(memory_space=pltpu.VMEM),
        scratch_shapes=[
            pltpu.VMEM((tokens, width), bf16),
            pltpu.VMEM((rows_kept, width), bf16),
            pltpu.VMEM((rows_kept, width), bf16),
            pltpu.VMEM(text_keys.shape, bf16),
            pltpu.VMEM(text_keys.shape, bf16),
            pltpu.SMEM((text_rows,), jnp.int32),
            pltpu.VMEM((HEAD_GROUPS, per_source, text_rows, HEAD_DIM), bf16),
            pltpu.VMEM((HEAD_GROUPS, text_rows, HEAD_DIM), bf16),
            pltpu.VMEM((tiles, HEAD_GROUPS * per_source + 1, text_rows, HEAD_DIM), bf16),
            pltpu.VMEM((2, rows_kept, width), bf16),
            pltpu.VMEM((2, rows_kept, width), bf16),
            pltpu.VMEM((head_count, tokens, HEAD_DIM), f32),
            pltpu.VMEM((head_count, tokens, HEAD_DIM), f32),
            pltpu.VMEM((head_count, tokens, HEAD_DIM), f32),
            pltpu.VMEM((2, tokens, rows_kept), bf16),
            pltpu.VMEM((2, tokens, HEAD_DIM), f32),
            dma((6,)),
            dma((HEAD_GROUPS, 2)),
            dma((HEAD_GROUPS, 2)),
            dma((2, tiles - 1)),
            dma((2, tiles - 1)),
            dma((2, head_count, 2)),
            dma((2, head_count, 2)),
        ],
        compiler_params=pltpu.CompilerParams(
            collective_id=0, has_side_effects=True, vmem_limit_bytes=56 * 1024 * 1024
        ),
        cost_estimate=pl.CostEstimate(
            flops=4 * tokens * keys_seen * width,
            bytes_accessed=10 * tokens * width,
            transcendentals=tokens * keys_seen * head_count,
        ),
    )(queries, keys, values, text_keys, text_values, text_mask)


def solution(mesh):
    tiles = mesh.shape["tile"] // HEAD_GROUPS

    def shards(*blocks):
        one_row = 1 < tiles <= 4 and blocks[3].shape[0] % 16 == 0
        return (row_shards if one_row else gathered_shards)(*blocks)

    return jax.shard_map(
        shards,
        mesh=mesh,
        in_specs=(
            P(("req", "tile"), None, None),
            P(("req", "tile"), None, None),
            P(("req", "tile"), None, None),
            P(("req", "tile"), None),
            P(("req", "tile"), None),
            P(("req", "tile")),
        ),
        out_specs=P(("req", "tile"), None, None),
        check_vma=False,
    )
```

```python
import functools
import math

import jax
import jax.numpy as jnp
from jax import lax
from jax.experimental import pallas as pl
from jax.experimental.pallas import tpu as pltpu
from jax.sharding import PartitionSpec as P

MESH = pl.DeviceIdType.MESH
EXP2_SCALE = math.log2(math.e) / math.sqrt(128)

TS = 8
HEAD_DIM = 128
HEAD_GROUPS = 4


MASKED = -1e30


def passed_along(value, axis, steps):
    count = lax.axis_size(axis)
    first, last = (max(0, -steps), min(count, count - steps))
    return lax.ppermute(value, axis, [(source, source + steps) for source in range(first, last)])


def shortened(value):
    return jax.tree.map(lambda a: a.astype(jnp.bfloat16) if a.dtype == jnp.float32 else a, value)


def fold_block(running, query_heads, key_block, value_block, key_keep):
    row_top, row_total, summed = running
    head_count = query_heads.shape[1]
    key_heads = key_block.reshape(key_block.shape[0], head_count, HEAD_DIM)
    value_heads = value_block.reshape(value_block.shape[0], head_count, HEAD_DIM)
    scores = jnp.einsum("qhd,khd->hqk", query_heads, key_heads, preferred_element_type=jnp.float32)
    scores = scores * (1.0 / math.sqrt(HEAD_DIM))
    scores = jnp.where(key_keep[None, None, :], scores, MASKED)
    new_top = jnp.maximum(row_top, jnp.max(scores, axis=-1))
    scale_down = jnp.exp(row_top - new_top)
    exp_terms = jnp.where(key_keep[None, None, :], jnp.exp(scores - new_top[:, :, None]), 0.0)
    row_total = row_total * scale_down + jnp.sum(exp_terms, axis=-1)
    weights = exp_terms.astype(jnp.bfloat16)
    summed = summed * scale_down[:, :, None] + jnp.einsum(
        "hqk,khd->hqd", weights, value_heads, preferred_element_type=jnp.float32
    )
    return (new_top, row_total, summed)


def gathered_shards(queries, keys, values, text_keys, text_values, text_mask):
    tokens = queries.shape[1]
    lane_width = queries.shape[2]
    head_count = lane_width // HEAD_DIM
    query_heads = queries[0].reshape(tokens, head_count, HEAD_DIM)
    own_pair = jnp.stack([keys[0], values[0]])
    group_count = HEAD_GROUPS
    tiles_all = lax.axis_size("tile") // group_count
    grid_w = min(4, tiles_all)
    grid_h = min(4, tiles_all // grid_w)
    grid_f = tiles_all // (grid_w * grid_h)
    frames_valid = grid_f * TS - TS // 4
    my_index = lax.axis_index("tile")
    tile_id = my_index // group_count
    head_group = my_index % group_count
    w_pos = tile_id % grid_w
    h_pos = tile_id // grid_w % grid_h
    f_pos = tile_id // (grid_w * grid_h)
    local_frame = jnp.arange(tokens, dtype=jnp.int32) // (TS * TS)

    def keep_mask(off_frame, off_height, off_width):
        inside = (
            (f_pos + off_frame >= 0)
            & (f_pos + off_frame < grid_f)
            & (h_pos + off_height >= 0)
            & (h_pos + off_height < grid_h)
            & (w_pos + off_width >= 0)
            & (w_pos + off_width < grid_w)
        )
        return inside & ((f_pos + off_frame) * TS + local_frame < frames_valid)

    running = (
        jnp.full((head_count, tokens), MASKED, jnp.float32),
        jnp.zeros((head_count, tokens), jnp.float32),
        jnp.zeros((head_count, tokens, HEAD_DIM), jnp.float32),
    )
    text_flags = text_mask.astype(jnp.bfloat16)
    piece_keys = lax.dynamic_slice_in_dim(
        lax.all_gather(text_keys, "tile", axis=0, tiled=True),
        head_group * lane_width,
        lane_width,
        1,
    )
    piece_values = lax.dynamic_slice_in_dim(
        lax.all_gather(text_values, "tile", axis=0, tiled=True),
        head_group * lane_width,
        lane_width,
        1,
    )
    running = fold_block(
        running,
        query_heads,
        piece_keys,
        piece_values,
        lax.all_gather(text_flags, "tile", axis=0, tiled=True) > 0.5,
    )
    running = fold_block(running, query_heads, own_pair[0], own_pair[1], keep_mask(0, 0, 0))
    width_set = {0: own_pair}
    for off_width in (-1, 1):
        width_set[off_width] = passed_along(own_pair, "tile", -off_width * group_count)
    width_offsets = sorted(width_set)
    row_stack = jnp.stack([width_set[spot] for spot in width_offsets])
    height_set = {0: row_stack}
    if grid_h > 1:
        for off_height in (-1, 1):
            height_set[off_height] = passed_along(
                shortened(row_stack), "tile", -off_height * grid_w * group_count
            ).astype(row_stack.dtype)
    height_offsets = sorted(height_set)
    slab_stack = jnp.stack([height_set[spot] for spot in height_offsets])

    def fold_slab(state_now, slab_pairs, off_frame):
        for h_slot, off_height in enumerate(height_offsets):
            for w_slot, off_width in enumerate(width_offsets):
                if off_frame == 0 and off_height == 0 and (off_width == 0):
                    continue
                state_now = fold_block(
                    state_now,
                    query_heads,
                    slab_pairs[h_slot, w_slot, 0],
                    slab_pairs[h_slot, w_slot, 1],
                    keep_mask(off_frame, off_height, off_width),
                )
        return state_now

    running = fold_slab(running, slab_stack, 0)
    if grid_f > 1:
        for off_frame in (-1, 1):
            got_slab = passed_along(
                shortened(slab_stack), "tile", -off_frame * grid_h * grid_w * group_count
            ).astype(slab_stack.dtype)
            running = fold_slab(running, got_slab, off_frame)
    row_top, row_total, summed = running
    result = summed / row_total[:, :, None]
    result = jnp.transpose(result, (1, 0, 2)).reshape(tokens, lane_width)
    return result.astype(jnp.bfloat16)[None]


def row_kernel(
    count, rows_kept, head_count, text_rows,
    q_hbm, k_hbm, v_hbm, tk_hbm, tv_hbm, mask_hbm, out_ref,
    q_ref, k_ref, v_ref, tk_ref, tv_ref, mask_ref, packets, flags_in, text, near_k, near_v,
    top_ref, total_ref, summed_ref, held_weights, held_top,
    in_sem, plane_send, plane_recv, block_send, block_recv, near_send, near_recv,
):
    groups = HEAD_GROUPS
    tiles = count // groups
    per_source = 2 * head_count
    flag_at = groups * per_source
    me = lax.axis_index("tile")
    tile = me // groups
    group = lax.rem(me, groups)
    first_here = tile * groups
    far = min(2, tiles - 1)

    def target(side, steps):
        return me + steps * groups if side == 0 else me - steps * groups

    def sends(side, steps=1):
        return tile + steps < tiles if side == 0 else tile >= steps

    def receives(side, steps=1):
        return sends(1 - side, steps)

    def partner(step):
        return first_here + lax.rem(group + step, groups)

    barrier = pltpu.get_barrier_semaphore()
    for step in range(1, groups):
        pl.semaphore_signal(barrier, inc=1, device_id={"tile": partner(step)}, device_id_type=MESH)
    partners = groups - 1
    for side in range(2):
        for steps in range(1, far + 1):
            partners += sends(side, steps).astype(jnp.int32)

            @pl.when(sends(side, steps))
            def _():
                pl.semaphore_signal(barrier, inc=1, device_id={"tile": target(side, steps)}, device_id_type=MESH)

    loads = [
        pltpu.make_async_copy(mask_hbm, mask_ref, in_sem.at[0]),
        pltpu.make_async_copy(tk_hbm, tk_ref, in_sem.at[1]),
        pltpu.make_async_copy(tv_hbm, tv_ref, in_sem.at[2]),
        pltpu.make_async_copy(q_hbm.at[0], q_ref, in_sem.at[3]),
        pltpu.make_async_copy(k_hbm.at[0, pl.ds(0, rows_kept), :], k_ref, in_sem.at[4]),
        pltpu.make_async_copy(v_hbm.at[0, pl.ds(0, rows_kept), :], v_ref, in_sem.at[5]),
    ]
    for load in loads:
        load.start()

    def near_copy(side, head, which):
        cols = pl.ds(head * HEAD_DIM, HEAD_DIM)
        source, landing = ((k_hbm, near_k), (v_hbm, near_v))[which]
        return pltpu.make_async_remote_copy(
            src_ref=source.at[0, pl.ds(0, rows_kept), cols],
            dst_ref=landing.at[side, :, cols],
            send_sem=near_send.at[side, head, which],
            recv_sem=near_recv.at[side, head, which],
            device_id={"tile": target(side, 1)},
            device_id_type=MESH,
        )

    def start_near(head, which):
        for side in range(2):

            @pl.when(sends(side))
            def _():
                near_copy(side, head, which).start()

    def plane_copies(step):
        to = partner(step)
        made = []
        for which, (source, landing) in enumerate(
            (
                (packets.at[lax.rem(group + step, groups)], text.at[tile, pl.ds(group * per_source, per_source)]),
                (flags_in.at[group], flags_in.at[group]),
            )
        ):
            made.append(
                pltpu.make_async_remote_copy(
                    src_ref=source,
                    dst_ref=landing,
                    send_sem=plane_send.at[step, which],
                    recv_sem=plane_recv.at[step, which],
                    device_id={"tile": to},
                    device_id_type=MESH,
                )
            )
        return made

    def block_copy(side, steps):
        relayed = steps > far
        owner = (tile - steps + 1 if side == 0 else tile + steps - 1) if relayed else tile
        return pltpu.make_async_remote_copy(
            src_ref=text.at[owner],
            dst_ref=text.at[owner],
            send_sem=block_send.at[side, steps - 1],
            recv_sem=block_recv.at[side, steps - 1],
            device_id={"tile": target(side, 1 if relayed else steps)},
            device_id_type=MESH,
        )

    def block_sent(side, steps):
        return sends(side) & receives(side, steps - 1) if steps > far else sends(side, steps)

    def start_block(steps):
        for side in range(2):

            @pl.when(block_sent(side, steps))
            def _():
                block_copy(side, steps).start()

    def wait_block(steps):
        for side in range(2):

            @pl.when(receives(side, steps))
            def _():
                owner = tile - steps if side == 0 else tile + steps
                pltpu.make_async_copy(text.at[owner], text.at[owner], block_recv.at[side, steps - 1]).wait()

    def weigh(head, keys, keep, first):
        query = q_ref[:, head * HEAD_DIM : (head + 1) * HEAD_DIM]
        scores = lax.dot_general(query, keys, (((1,), (1,)), ((), ())), preferred_element_type=jnp.float32)
        if keep is not None:
            scores = jnp.where(keep, scores, MASKED)
        block_top = jnp.broadcast_to(jnp.max(scores, axis=1, keepdims=True), (scores.shape[0], HEAD_DIM))
        new_top = block_top if first else jnp.maximum(top_ref[head], block_top)
        pieces = [
            jnp.exp2((scores[:, at : at + HEAD_DIM] - new_top) * EXP2_SCALE) for at in range(0, keys.shape[0], HEAD_DIM)
        ]
        part = functools.reduce(lambda a, b: a + b, pieces)
        weights = jnp.concatenate([piece.astype(jnp.bfloat16) for piece in pieces], axis=1)
        if first:
            total_ref[head] = part
            summed = None
        else:
            scale_down = jnp.exp2((top_ref[head] - new_top) * EXP2_SCALE)
            total_ref[head] = total_ref[head] * scale_down + part
            summed = summed_ref[head] * scale_down
        top_ref[head] = new_top
        return weights, summed

    def fold(head, keys, values, keep, first):
        weights, summed = weigh(head, keys, keep, first)
        product = jnp.dot(weights, values, preferred_element_type=jnp.float32)
        summed_ref[head] = product if summed is None else summed + product

    def head_cols(head):
        return slice(head * HEAD_DIM, (head + 1) * HEAD_DIM)

    def fold_near(head):
        cols = head_cols(head)
        for side in range(2):

            @pl.when(receives(side))
            def _():
                for which in range(2):
                    near_copy(side, head, which).wait_recv()
                fold(head, near_k[side, :, cols], near_v[side, :, cols], None, False)

    def weigh_near(head):
        for side in range(2):

            @pl.when(receives(side))
            def _():
                near_copy(side, head, 0).wait_recv()
                weights, summed = weigh(head, near_k[side, :, head_cols(head)], None, False)
                summed_ref[head] = summed
                held_weights[side] = weights
                held_top[side] = top_ref[head]

    def apply_near(head):
        for side in range(2):

            @pl.when(receives(side))
            def _():
                near_copy(side, head, 1).wait_recv()
                product = jnp.dot(
                    held_weights[side], near_v[side, :, head_cols(head)], preferred_element_type=jnp.float32
                )
                since = jnp.exp2((held_top[side] - top_ref[head]) * EXP2_SCALE)
                summed_ref[head] = summed_ref[head] + product * since

    def finish(head):
        total = jnp.sum(total_ref[head], axis=1, keepdims=True)
        out_ref[0, :, head_cols(head)] = (summed_ref[head] / total).astype(out_ref.dtype)

    def fold_own(head):
        fold(head, k_ref[:, head_cols(head)], v_ref[:, head_cols(head)], None, True)

    pl.semaphore_wait(barrier, partners)
    waiting = [(head, which) for head in range(head_count) for which in range(2)]
    start_near(*waiting[0])

    loads[0].wait()
    row_of = lax.broadcasted_iota(jnp.int32, (text_rows, HEAD_DIM), 0)
    lane_of = lax.broadcasted_iota(jnp.int32, (text_rows, HEAD_DIM), 1)
    flags = jnp.zeros((text_rows, HEAD_DIM), jnp.float32)
    for row in range(text_rows):
        flags = jnp.where((row_of == row) & (lane_of == me), mask_ref[row].astype(jnp.float32), flags)
    flags_in[group] = flags.astype(jnp.bfloat16)
    loads[1].wait()
    loads[2].wait()
    for to in range(groups):
        for which, source in enumerate((tk_ref, tv_ref)):
            for head in range(head_count):
                at = (to * head_count + head) * HEAD_DIM
                packets[to, which * head_count + head] = source[:, at : at + HEAD_DIM]
    text[tile, pl.ds(group * per_source, per_source)] = packets[group]
    for step in range(1, groups):
        for copy in plane_copies(step):
            copy.start()
    for load in loads[3:]:
        load.wait()
    fold_own(0)
    for step in range(1, groups):
        for copy in plane_copies(step):
            copy.wait_recv()
    text[tile, flag_at] = functools.reduce(lambda a, b: a + b, [flags_in[source] for source in range(groups)])

    for steps in range(1, far + 1):
        start_block(steps)
    for item in waiting[1:4]:
        start_near(*item)
    for head in range(1, head_count):
        fold_own(head)
    wait_block(far)
    for steps in range(far + 1, tiles):
        start_block(steps)
    for item in waiting[4:]:
        start_near(*item)
    for head in range(head_count - 1):
        fold_near(head)
    for steps in range(1, tiles):
        if steps != far:
            wait_block(steps)

    wide_row = lax.broadcasted_iota(jnp.int32, (count * text_rows, HEAD_DIM), 0)
    wide_lane = lax.broadcasted_iota(jnp.int32, (count * text_rows, HEAD_DIM), 1)
    spread = jnp.concatenate([text[source // groups, flag_at] for source in range(count)], axis=0)
    spread = jnp.where(wide_lane == wide_row // text_rows, spread, jnp.zeros_like(spread))
    keep_row = lax.dot_general(
        jnp.ones((8, HEAD_DIM), jnp.bfloat16), spread, (((1,), (1,)), ((), ())), preferred_element_type=jnp.float32
    )[0:1, :]
    keep = jnp.broadcast_to(keep_row, (q_ref.shape[0], keep_row.shape[1])) > 0.5

    def text_piece(at):
        return jnp.concatenate(
            [text[source // groups, source % groups * per_source + at] for source in range(count)], axis=0
        )

    for head in range(head_count):
        fold(head, text_piece(head), text_piece(head_count + head), keep, False)
        if head == head_count - 1:
            weigh_near(head)
            apply_near(head)
        finish(head)

    for step in range(1, groups):
        for copy in plane_copies(step):
            copy.wait_send()
    for side in range(2):

        @pl.when(sends(side))
        def _():
            for head in range(head_count):
                for which in range(2):
                    near_copy(side, head, which).wait_send()

        for steps in range(1, tiles):

            @pl.when(block_sent(side, steps))
            def _():
                block_copy(side, steps).wait_send()


def row_shards(queries, keys, values, text_keys, text_values, text_mask):
    tokens, width = queries.shape[1:]
    head_count = width // HEAD_DIM
    count = lax.axis_size("tile")
    tiles = count // HEAD_GROUPS
    text_rows = text_keys.shape[0]
    rows_kept = (TS - TS // 4) * TS * TS
    bf16, f32 = jnp.bfloat16, jnp.float32
    dma = pltpu.SemaphoreType.DMA
    hbm = pl.BlockSpec(memory_space=pltpu.HBM)
    keys_seen = 3 * rows_kept + count * text_rows
    per_source = 2 * head_count
    return pl.pallas_call(
        functools.partial(row_kernel, count, rows_kept, head_count, text_rows),
        out_shape=pltpu.VMEM(queries.shape, bf16),
        in_specs=[hbm] * 6,
        out_specs=pl.BlockSpec(memory_space=pltpu.VMEM),
        scratch_shapes=[
            pltpu.VMEM((tokens, width), bf16),
            pltpu.VMEM((rows_kept, width), bf16),
            pltpu.VMEM((rows_kept, width), bf16),
            pltpu.VMEM(text_keys.shape, bf16),
            pltpu.VMEM(text_keys.shape, bf16),
            pltpu.SMEM((text_rows,), jnp.int32),
            pltpu.VMEM((HEAD_GROUPS, per_source, text_rows, HEAD_DIM), bf16),
            pltpu.VMEM((HEAD_GROUPS, text_rows, HEAD_DIM), bf16),
            pltpu.VMEM((tiles, HEAD_GROUPS * per_source + 1, text_rows, HEAD_DIM), bf16),
            pltpu.VMEM((2, rows_kept, width), bf16),
            pltpu.VMEM((2, rows_kept, width), bf16),
            pltpu.VMEM((head_count, tokens, HEAD_DIM), f32),
            pltpu.VMEM((head_count, tokens, HEAD_DIM), f32),
            pltpu.VMEM((head_count, tokens, HEAD_DIM), f32),
            pltpu.VMEM((2, tokens, rows_kept), bf16),
            pltpu.VMEM((2, tokens, HEAD_DIM), f32),
            dma((6,)),
            dma((HEAD_GROUPS, 2)),
            dma((HEAD_GROUPS, 2)),
            dma((2, tiles - 1)),
            dma((2, tiles - 1)),
            dma((2, head_count, 2)),
            dma((2, head_count, 2)),
        ],
        compiler_params=pltpu.CompilerParams(
            collective_id=0, has_side_effects=True, vmem_limit_bytes=56 * 1024 * 1024
        ),
        cost_estimate=pl.CostEstimate(
            flops=4 * tokens * keys_seen * width,
            bytes_accessed=10 * tokens * width,
            transcendentals=tokens * keys_seen * head_count,
        ),
    )(queries, keys, values, text_keys, text_values, text_mask)


def solution(mesh):
    tiles = mesh.shape["tile"] // HEAD_GROUPS

    def shards(*blocks):
        one_row = 1 < tiles <= 4 and blocks[3].shape[0] % 16 == 0
        return (row_shards if one_row else gathered_shards)(*blocks)

    return jax.shard_map(
        shards,
        mesh=mesh,
        in_specs=(
            P(("req", "tile"), None, None),
            P(("req", "tile"), None, None),
            P(("req", "tile"), None, None),
            P(("req", "tile"), None),
            P(("req", "tile"), None),
            P(("req", "tile")),
        ),
        out_specs=P(("req", "tile"), None, None),
        check_vma=False,
    )
```

```python
import functools
import math

import jax
import jax.numpy as jnp
from jax import lax
from jax.experimental import pallas as pl
from jax.experimental.pallas import tpu as pltpu
from jax.sharding import PartitionSpec as P

MESH = pl.DeviceIdType.MESH
EXP2_SCALE = math.log2(math.e) / math.sqrt(128)

TS = 8
HEAD_DIM = 128
HEAD_GROUPS = 4


MASKED = -1e30


def passed_along(value, axis, steps):
    count = lax.axis_size(axis)
    first, last = (max(0, -steps), min(count, count - steps))
    return lax.ppermute(value, axis, [(source, source + steps) for source in range(first, last)])


def shortened(value):
    return jax.tree.map(lambda a: a.astype(jnp.bfloat16) if a.dtype == jnp.float32 else a, value)


def fold_block(running, query_heads, key_block, value_block, key_keep):
    row_top, row_total, summed = running
    head_count = query_heads.shape[1]
    key_heads = key_block.reshape(key_block.shape[0], head_count, HEAD_DIM)
    value_heads = value_block.reshape(value_block.shape[0], head_count, HEAD_DIM)
    scores = jnp.einsum("qhd,khd->hqk", query_heads, key_heads, preferred_element_type=jnp.float32)
    scores = scores * (1.0 / math.sqrt(HEAD_DIM))
    scores = jnp.where(key_keep[None, None, :], scores, MASKED)
    new_top = jnp.maximum(row_top, jnp.max(scores, axis=-1))
    scale_down = jnp.exp(row_top - new_top)
    exp_terms = jnp.where(key_keep[None, None, :], jnp.exp(scores - new_top[:, :, None]), 0.0)
    row_total = row_total * scale_down + jnp.sum(exp_terms, axis=-1)
    weights = exp_terms.astype(jnp.bfloat16)
    summed = summed * scale_down[:, :, None] + jnp.einsum(
        "hqk,khd->hqd", weights, value_heads, preferred_element_type=jnp.float32
    )
    return (new_top, row_total, summed)


def gathered_shards(queries, keys, values, text_keys, text_values, text_mask):
    tokens = queries.shape[1]
    lane_width = queries.shape[2]
    head_count = lane_width // HEAD_DIM
    query_heads = queries[0].reshape(tokens, head_count, HEAD_DIM)
    own_pair = jnp.stack([keys[0], values[0]])
    group_count = HEAD_GROUPS
    tiles_all = lax.axis_size("tile") // group_count
    grid_w = min(4, tiles_all)
    grid_h = min(4, tiles_all // grid_w)
    grid_f = tiles_all // (grid_w * grid_h)
    frames_valid = grid_f * TS - TS // 4
    my_index = lax.axis_index("tile")
    tile_id = my_index // group_count
    head_group = my_index % group_count
    w_pos = tile_id % grid_w
    h_pos = tile_id // grid_w % grid_h
    f_pos = tile_id // (grid_w * grid_h)
    local_frame = jnp.arange(tokens, dtype=jnp.int32) // (TS * TS)

    def keep_mask(off_frame, off_height, off_width):
        inside = (
            (f_pos + off_frame >= 0)
            & (f_pos + off_frame < grid_f)
            & (h_pos + off_height >= 0)
            & (h_pos + off_height < grid_h)
            & (w_pos + off_width >= 0)
            & (w_pos + off_width < grid_w)
        )
        return inside & ((f_pos + off_frame) * TS + local_frame < frames_valid)

    running = (
        jnp.full((head_count, tokens), MASKED, jnp.float32),
        jnp.zeros((head_count, tokens), jnp.float32),
        jnp.zeros((head_count, tokens, HEAD_DIM), jnp.float32),
    )
    text_flags = text_mask.astype(jnp.bfloat16)
    piece_keys = lax.dynamic_slice_in_dim(
        lax.all_gather(text_keys, "tile", axis=0, tiled=True),
        head_group * lane_width,
        lane_width,
        1,
    )
    piece_values = lax.dynamic_slice_in_dim(
        lax.all_gather(text_values, "tile", axis=0, tiled=True),
        head_group * lane_width,
        lane_width,
        1,
    )
    running = fold_block(
        running,
        query_heads,
        piece_keys,
        piece_values,
        lax.all_gather(text_flags, "tile", axis=0, tiled=True) > 0.5,
    )
    running = fold_block(running, query_heads, own_pair[0], own_pair[1], keep_mask(0, 0, 0))
    width_set = {0: own_pair}
    for off_width in (-1, 1):
        width_set[off_width] = passed_along(own_pair, "tile", -off_width * group_count)
    width_offsets = sorted(width_set)
    row_stack = jnp.stack([width_set[spot] for spot in width_offsets])
    height_set = {0: row_stack}
    if grid_h > 1:
        for off_height in (-1, 1):
            height_set[off_height] = passed_along(
                shortened(row_stack), "tile", -off_height * grid_w * group_count
            ).astype(row_stack.dtype)
    height_offsets = sorted(height_set)
    slab_stack = jnp.stack([height_set[spot] for spot in height_offsets])

    def fold_slab(state_now, slab_pairs, off_frame):
        for h_slot, off_height in enumerate(height_offsets):
            for w_slot, off_width in enumerate(width_offsets):
                if off_frame == 0 and off_height == 0 and (off_width == 0):
                    continue
                state_now = fold_block(
                    state_now,
                    query_heads,
                    slab_pairs[h_slot, w_slot, 0],
                    slab_pairs[h_slot, w_slot, 1],
                    keep_mask(off_frame, off_height, off_width),
                )
        return state_now

    running = fold_slab(running, slab_stack, 0)
    if grid_f > 1:
        for off_frame in (-1, 1):
            got_slab = passed_along(
                shortened(slab_stack), "tile", -off_frame * grid_h * grid_w * group_count
            ).astype(slab_stack.dtype)
            running = fold_slab(running, got_slab, off_frame)
    row_top, row_total, summed = running
    result = summed / row_total[:, :, None]
    result = jnp.transpose(result, (1, 0, 2)).reshape(tokens, lane_width)
    return result.astype(jnp.bfloat16)[None]


def row_kernel(
    count, rows_kept, head_count, text_rows,
    q_hbm, k_hbm, v_hbm, tk_hbm, tv_hbm, mask_hbm, out_ref,
    q_ref, k_ref, v_ref, tk_ref, tv_ref, mask_ref, packets, flags_in, text, near_k, near_v,
    top_ref, total_ref, summed_ref, held_weights, held_top,
    in_sem, plane_send, plane_recv, chain_send, chain_recv, near_send, near_recv,
):
    groups = HEAD_GROUPS
    tiles = count // groups
    per_source = 2 * head_count
    flag_at = groups * per_source
    me = lax.axis_index("tile")
    tile = me // groups
    group = lax.rem(me, groups)
    first_here = tile * groups
    has_left = tile > 0
    has_right = tile < tiles - 1
    target = (me + groups, me - groups)
    sends = (has_right, has_left)
    receives = (has_left, has_right)

    def partner(step):
        return first_here + lax.rem(group + step, groups)

    barrier = pltpu.get_barrier_semaphore()
    for step in range(1, groups):
        pl.semaphore_signal(barrier, inc=1, device_id={"tile": partner(step)}, device_id_type=MESH)
    for side in range(2):

        @pl.when(sends[side])
        def _():
            pl.semaphore_signal(barrier, inc=1, device_id={"tile": target[side]}, device_id_type=MESH)

    loads = [
        pltpu.make_async_copy(mask_hbm, mask_ref, in_sem.at[0]),
        pltpu.make_async_copy(tk_hbm, tk_ref, in_sem.at[1]),
        pltpu.make_async_copy(tv_hbm, tv_ref, in_sem.at[2]),
        pltpu.make_async_copy(q_hbm.at[0], q_ref, in_sem.at[3]),
    ]
    for which, (source, landing) in enumerate(((k_hbm, k_ref), (v_hbm, v_ref))):
        for head in range(head_count):
            cols = pl.ds(head * HEAD_DIM, HEAD_DIM)
            loads.append(
                pltpu.make_async_copy(
                    source.at[0, pl.ds(0, rows_kept), cols], landing.at[head], in_sem.at[4 + which * head_count + head]
                )
            )
    for load in loads:
        load.start()

    def near_copy(side, head, which):
        source, landing = ((k_ref, near_k), (v_ref, near_v))[which]
        return pltpu.make_async_remote_copy(
            src_ref=source.at[head],
            dst_ref=landing.at[side, head],
            send_sem=near_send.at[side, head, which],
            recv_sem=near_recv.at[side, head, which],
            device_id={"tile": target[side]},
            device_id_type=MESH,
        )

    def start_near(head, which):
        for side in range(2):

            @pl.when(sends[side])
            def _():
                near_copy(side, head, which).start()

    def plane_copies(step):
        to = partner(step)
        made = []
        for which, (source, landing) in enumerate(
            (
                (packets.at[lax.rem(group + step, groups)], text.at[tile, pl.ds(group * per_source, per_source)]),
                (flags_in.at[group], flags_in.at[group]),
            )
        ):
            made.append(
                pltpu.make_async_remote_copy(
                    src_ref=source,
                    dst_ref=landing,
                    send_sem=plane_send.at[step, which],
                    recv_sem=plane_recv.at[step, which],
                    device_id={"tile": to},
                    device_id_type=MESH,
                )
            )
        return made

    def chain_copy(side, hop, owner):
        return pltpu.make_async_remote_copy(
            src_ref=text.at[owner],
            dst_ref=text.at[owner],
            send_sem=chain_send.at[side, hop],
            recv_sem=chain_recv.at[side, hop],
            device_id={"tile": target[side]},
            device_id_type=MESH,
        )

    def chain_sent(side, hop):
        owner = tile - hop if side == 0 else tile + hop
        there = owner >= 0 if side == 0 else owner < tiles
        return owner, there & sends[side]

    def chain_got(side, hop):
        owner = tile - hop - 1 if side == 0 else tile + hop + 1
        return owner, owner >= 0 if side == 0 else owner < tiles

    def start_chain(hop):
        for side in range(2):
            owner, there = chain_sent(side, hop)

            @pl.when(there)
            def _():
                chain_copy(side, hop, owner).start()

    def wait_chain(hop):
        for side in range(2):
            owner, there = chain_got(side, hop)

            @pl.when(there)
            def _():
                chain_copy(side, hop, owner).wait_recv()

    def weigh(head, keys, keep, first):
        query = q_ref[:, head * HEAD_DIM : (head + 1) * HEAD_DIM]
        scores = lax.dot_general(query, keys, (((1,), (1,)), ((), ())), preferred_element_type=jnp.float32)
        if keep is not None:
            scores = jnp.where(keep, scores, MASKED)
        block_top = jnp.broadcast_to(jnp.max(scores, axis=1, keepdims=True), (scores.shape[0], HEAD_DIM))
        new_top = block_top if first else jnp.maximum(top_ref[head], block_top)
        pieces = [
            jnp.exp2((scores[:, at : at + HEAD_DIM] - new_top) * EXP2_SCALE) for at in range(0, keys.shape[0], HEAD_DIM)
        ]
        part = functools.reduce(lambda a, b: a + b, pieces)
        weights = jnp.concatenate([piece.astype(jnp.bfloat16) for piece in pieces], axis=1)
        if first:
            total_ref[head] = part
            summed = None
        else:
            scale_down = jnp.exp2((top_ref[head] - new_top) * EXP2_SCALE)
            total_ref[head] = total_ref[head] * scale_down + part
            summed = summed_ref[head] * scale_down
        top_ref[head] = new_top
        return weights, summed

    def fold(head, keys, values, keep, first):
        weights, summed = weigh(head, keys, keep, first)
        product = jnp.dot(weights, values, preferred_element_type=jnp.float32)
        summed_ref[head] = product if summed is None else summed + product

    def head_cols(head):
        return slice(head * HEAD_DIM, (head + 1) * HEAD_DIM)

    def fold_near(head):
        for side in range(2):

            @pl.when(receives[side])
            def _():
                for which in range(2):
                    near_copy(side, head, which).wait_recv()
                fold(head, near_k[side, head], near_v[side, head], None, False)

    def weigh_near(head):
        for side in range(2):

            @pl.when(receives[side])
            def _():
                near_copy(side, head, 0).wait_recv()
                weights, summed = weigh(head, near_k[side, head], None, False)
                summed_ref[head] = summed
                held_weights[side] = weights
                held_top[side] = top_ref[head]

    def apply_near(head):
        for side in range(2):

            @pl.when(receives[side])
            def _():
                near_copy(side, head, 1).wait_recv()
                product = jnp.dot(
                    held_weights[side], near_v[side, head], preferred_element_type=jnp.float32
                )
                since = jnp.exp2((held_top[side] - top_ref[head]) * EXP2_SCALE)
                summed_ref[head] = summed_ref[head] + product * since

    def finish(head):
        total = jnp.sum(total_ref[head], axis=1, keepdims=True)
        out_ref[0, :, head_cols(head)] = (summed_ref[head] / total).astype(out_ref.dtype)

    def fold_own(head):
        fold(head, k_ref[head], v_ref[head], None, True)

    pl.semaphore_wait(barrier, groups - 1 + has_left.astype(jnp.int32) + has_right.astype(jnp.int32))
    waiting = [(head, which) for head in range(head_count) for which in range(2)]
    for load in loads[3:]:
        load.wait()
    start_near(*waiting[0])

    loads[0].wait()
    row_of = lax.broadcasted_iota(jnp.int32, (text_rows, HEAD_DIM), 0)
    lane_of = lax.broadcasted_iota(jnp.int32, (text_rows, HEAD_DIM), 1)
    flags = jnp.zeros((text_rows, HEAD_DIM), jnp.float32)
    for row in range(text_rows):
        flags = jnp.where((row_of == row) & (lane_of == me), mask_ref[row].astype(jnp.float32), flags)
    flags_in[group] = flags.astype(jnp.bfloat16)
    loads[1].wait()
    loads[2].wait()
    for to in range(groups):
        for which, source in enumerate((tk_ref, tv_ref)):
            for head in range(head_count):
                at = (to * head_count + head) * HEAD_DIM
                packets[to, which * head_count + head] = source[:, at : at + HEAD_DIM]
    text[tile, pl.ds(group * per_source, per_source)] = packets[group]
    for step in range(1, groups):
        for copy in plane_copies(step):
            copy.start()
    fold_own(0)
    for step in range(1, groups):
        for copy in plane_copies(step):
            copy.wait_recv()
    text[tile, flag_at] = functools.reduce(lambda a, b: a + b, [flags_in[source] for source in range(groups)])

    start_chain(0)
    for item in waiting[1:3]:
        start_near(*item)
    for head in range(1, head_count):
        fold_own(head)
    for hop in range(1, tiles - 1):
        wait_chain(hop - 1)
        start_chain(hop)
        start_near(*waiting[2 + hop])
        if hop == 1:
            fold_near(0)
    for item in waiting[1 + tiles :]:
        start_near(*item)
    for head in range(1 if tiles > 2 else 0, head_count - 1):
        fold_near(head)
    wait_chain(tiles - 2)

    wide_row = lax.broadcasted_iota(jnp.int32, (count * text_rows, HEAD_DIM), 0)
    wide_lane = lax.broadcasted_iota(jnp.int32, (count * text_rows, HEAD_DIM), 1)
    spread = jnp.concatenate([text[source // groups, flag_at] for source in range(count)], axis=0)
    spread = jnp.where(wide_lane == wide_row // text_rows, spread, jnp.zeros_like(spread))
    keep_row = lax.dot_general(
        jnp.ones((8, HEAD_DIM), jnp.bfloat16), spread, (((1,), (1,)), ((), ())), preferred_element_type=jnp.float32
    )[0:1, :]
    keep = jnp.broadcast_to(keep_row, (q_ref.shape[0], keep_row.shape[1])) > 0.5

    def text_piece(at):
        return jnp.concatenate(
            [text[source // groups, source % groups * per_source + at] for source in range(count)], axis=0
        )

    for head in range(head_count):
        fold(head, text_piece(head), text_piece(head_count + head), keep, False)
        if head == head_count - 1:
            weigh_near(head)
            apply_near(head)
        finish(head)

    for step in range(1, groups):
        for copy in plane_copies(step):
            copy.wait_send()
    for side in range(2):

        @pl.when(sends[side])
        def _():
            for head in range(head_count):
                for which in range(2):
                    near_copy(side, head, which).wait_send()

        for hop in range(tiles - 1):
            owner, there = chain_sent(side, hop)

            @pl.when(there)
            def _():
                chain_copy(side, hop, owner).wait_send()


def row_shards(queries, keys, values, text_keys, text_values, text_mask):
    tokens, width = queries.shape[1:]
    head_count = width // HEAD_DIM
    count = lax.axis_size("tile")
    tiles = count // HEAD_GROUPS
    text_rows = text_keys.shape[0]
    rows_kept = (TS - TS // 4) * TS * TS
    bf16, f32 = jnp.bfloat16, jnp.float32
    dma = pltpu.SemaphoreType.DMA
    hbm = pl.BlockSpec(memory_space=pltpu.HBM)
    keys_seen = 3 * rows_kept + count * text_rows
    per_source = 2 * head_count
    return pl.pallas_call(
        functools.partial(row_kernel, count, rows_kept, head_count, text_rows),
        out_shape=pltpu.VMEM(queries.shape, bf16),
        in_specs=[hbm] * 6,
        out_specs=pl.BlockSpec(memory_space=pltpu.VMEM),
        scratch_shapes=[
            pltpu.VMEM((tokens, width), bf16),
            pltpu.VMEM((head_count, rows_kept, HEAD_DIM), bf16),
            pltpu.VMEM((head_count, rows_kept, HEAD_DIM), bf16),
            pltpu.VMEM(text_keys.shape, bf16),
            pltpu.VMEM(text_keys.shape, bf16),
            pltpu.SMEM((text_rows,), jnp.int32),
            pltpu.VMEM((HEAD_GROUPS, per_source, text_rows, HEAD_DIM), bf16),
            pltpu.VMEM((HEAD_GROUPS, text_rows, HEAD_DIM), bf16),
            pltpu.VMEM((tiles, HEAD_GROUPS * per_source + 1, text_rows, HEAD_DIM), bf16),
            pltpu.VMEM((2, head_count, rows_kept, HEAD_DIM), bf16),
            pltpu.VMEM((2, head_count, rows_kept, HEAD_DIM), bf16),
            pltpu.VMEM((head_count, tokens, HEAD_DIM), f32),
            pltpu.VMEM((head_count, tokens, HEAD_DIM), f32),
            pltpu.VMEM((head_count, tokens, HEAD_DIM), f32),
            pltpu.VMEM((2, tokens, rows_kept), bf16),
            pltpu.VMEM((2, tokens, HEAD_DIM), f32),
            dma((4 + 2 * head_count,)),
            dma((HEAD_GROUPS, 2)),
            dma((HEAD_GROUPS, 2)),
            dma((2, tiles - 1)),
            dma((2, tiles - 1)),
            dma((2, head_count, 2)),
            dma((2, head_count, 2)),
        ],
        compiler_params=pltpu.CompilerParams(
            collective_id=0, has_side_effects=True, vmem_limit_bytes=56 * 1024 * 1024
        ),
        cost_estimate=pl.CostEstimate(
            flops=4 * tokens * keys_seen * width,
            bytes_accessed=10 * tokens * width,
            transcendentals=tokens * keys_seen * head_count,
        ),
    )(queries, keys, values, text_keys, text_values, text_mask)


def solution(mesh):
    tiles = mesh.shape["tile"] // HEAD_GROUPS

    def shards(*blocks):
        one_row = 1 < tiles <= 4 and blocks[3].shape[0] % 16 == 0
        return (row_shards if one_row else gathered_shards)(*blocks)

    return jax.shard_map(
        shards,
        mesh=mesh,
        in_specs=(
            P(("req", "tile"), None, None),
            P(("req", "tile"), None, None),
            P(("req", "tile"), None, None),
            P(("req", "tile"), None),
            P(("req", "tile"), None),
            P(("req", "tile")),
        ),
        out_specs=P(("req", "tile"), None, None),
        check_vma=False,
    )
```

```python
import functools
import math

import jax
import jax.numpy as jnp
from jax import lax
from jax.experimental import pallas as pl
from jax.experimental.pallas import tpu as pltpu
from jax.sharding import PartitionSpec as P

MESH = pl.DeviceIdType.MESH
EXP2_SCALE = math.log2(math.e) / math.sqrt(128)

TS = 8
HEAD_DIM = 128
HEAD_GROUPS = 4


MASKED = -1e30


def passed_along(value, axis, steps):
    count = lax.axis_size(axis)
    first, last = (max(0, -steps), min(count, count - steps))
    return lax.ppermute(value, axis, [(source, source + steps) for source in range(first, last)])


def shortened(value):
    return jax.tree.map(lambda a: a.astype(jnp.bfloat16) if a.dtype == jnp.float32 else a, value)


def fold_block(running, query_heads, key_block, value_block, key_keep):
    row_top, row_total, summed = running
    head_count = query_heads.shape[1]
    key_heads = key_block.reshape(key_block.shape[0], head_count, HEAD_DIM)
    value_heads = value_block.reshape(value_block.shape[0], head_count, HEAD_DIM)
    scores = jnp.einsum("qhd,khd->hqk", query_heads, key_heads, preferred_element_type=jnp.float32)
    scores = scores * (1.0 / math.sqrt(HEAD_DIM))
    scores = jnp.where(key_keep[None, None, :], scores, MASKED)
    new_top = jnp.maximum(row_top, jnp.max(scores, axis=-1))
    scale_down = jnp.exp(row_top - new_top)
    exp_terms = jnp.where(key_keep[None, None, :], jnp.exp(scores - new_top[:, :, None]), 0.0)
    row_total = row_total * scale_down + jnp.sum(exp_terms, axis=-1)
    weights = exp_terms.astype(jnp.bfloat16)
    summed = summed * scale_down[:, :, None] + jnp.einsum(
        "hqk,khd->hqd", weights, value_heads, preferred_element_type=jnp.float32
    )
    return (new_top, row_total, summed)


def gathered_shards(queries, keys, values, text_keys, text_values, text_mask):
    tokens = queries.shape[1]
    lane_width = queries.shape[2]
    head_count = lane_width // HEAD_DIM
    query_heads = queries[0].reshape(tokens, head_count, HEAD_DIM)
    own_pair = jnp.stack([keys[0], values[0]])
    group_count = HEAD_GROUPS
    tiles_all = lax.axis_size("tile") // group_count
    grid_w = min(4, tiles_all)
    grid_h = min(4, tiles_all // grid_w)
    grid_f = tiles_all // (grid_w * grid_h)
    frames_valid = grid_f * TS - TS // 4
    my_index = lax.axis_index("tile")
    tile_id = my_index // group_count
    head_group = my_index % group_count
    w_pos = tile_id % grid_w
    h_pos = tile_id // grid_w % grid_h
    f_pos = tile_id // (grid_w * grid_h)
    local_frame = jnp.arange(tokens, dtype=jnp.int32) // (TS * TS)

    def keep_mask(off_frame, off_height, off_width):
        inside = (
            (f_pos + off_frame >= 0)
            & (f_pos + off_frame < grid_f)
            & (h_pos + off_height >= 0)
            & (h_pos + off_height < grid_h)
            & (w_pos + off_width >= 0)
            & (w_pos + off_width < grid_w)
        )
        return inside & ((f_pos + off_frame) * TS + local_frame < frames_valid)

    running = (
        jnp.full((head_count, tokens), MASKED, jnp.float32),
        jnp.zeros((head_count, tokens), jnp.float32),
        jnp.zeros((head_count, tokens, HEAD_DIM), jnp.float32),
    )
    text_flags = text_mask.astype(jnp.bfloat16)
    piece_keys = lax.dynamic_slice_in_dim(
        lax.all_gather(text_keys, "tile", axis=0, tiled=True),
        head_group * lane_width,
        lane_width,
        1,
    )
    piece_values = lax.dynamic_slice_in_dim(
        lax.all_gather(text_values, "tile", axis=0, tiled=True),
        head_group * lane_width,
        lane_width,
        1,
    )
    running = fold_block(
        running,
        query_heads,
        piece_keys,
        piece_values,
        lax.all_gather(text_flags, "tile", axis=0, tiled=True) > 0.5,
    )
    running = fold_block(running, query_heads, own_pair[0], own_pair[1], keep_mask(0, 0, 0))
    width_set = {0: own_pair}
    for off_width in (-1, 1):
        width_set[off_width] = passed_along(own_pair, "tile", -off_width * group_count)
    width_offsets = sorted(width_set)
    row_stack = jnp.stack([width_set[spot] for spot in width_offsets])
    height_set = {0: row_stack}
    if grid_h > 1:
        for off_height in (-1, 1):
            height_set[off_height] = passed_along(
                shortened(row_stack), "tile", -off_height * grid_w * group_count
            ).astype(row_stack.dtype)
    height_offsets = sorted(height_set)
    slab_stack = jnp.stack([height_set[spot] for spot in height_offsets])

    def fold_slab(state_now, slab_pairs, off_frame):
        for h_slot, off_height in enumerate(height_offsets):
            for w_slot, off_width in enumerate(width_offsets):
                if off_frame == 0 and off_height == 0 and (off_width == 0):
                    continue
                state_now = fold_block(
                    state_now,
                    query_heads,
                    slab_pairs[h_slot, w_slot, 0],
                    slab_pairs[h_slot, w_slot, 1],
                    keep_mask(off_frame, off_height, off_width),
                )
        return state_now

    running = fold_slab(running, slab_stack, 0)
    if grid_f > 1:
        for off_frame in (-1, 1):
            got_slab = passed_along(
                shortened(slab_stack), "tile", -off_frame * grid_h * grid_w * group_count
            ).astype(slab_stack.dtype)
            running = fold_slab(running, got_slab, off_frame)
    row_top, row_total, summed = running
    result = summed / row_total[:, :, None]
    result = jnp.transpose(result, (1, 0, 2)).reshape(tokens, lane_width)
    return result.astype(jnp.bfloat16)[None]


def row_kernel(
    count, rows_kept, head_count, text_rows,
    q_hbm, k_hbm, v_hbm, tk_hbm, tv_hbm, mask_hbm, out_ref,
    q_ref, own, tk_ref, tv_ref, mask_ref, packets, flags_in, text, near,
    top_ref, total_ref, summed_ref,
    in_sem, plane_send, plane_recv, chain_send, chain_recv, near_send, near_recv,
):
    groups = HEAD_GROUPS
    tiles = count // groups
    per_source = 2 * head_count
    flag_at = groups * per_source
    me = lax.axis_index("tile")
    tile = me // groups
    group = lax.rem(me, groups)
    first_here = tile * groups
    has_left = tile > 0
    has_right = tile < tiles - 1
    target = (me + groups, me - groups)
    sends = (has_right, has_left)
    receives = (has_left, has_right)

    def partner(step):
        return first_here + lax.rem(group + step, groups)

    barrier = pltpu.get_barrier_semaphore()
    for step in range(1, groups):
        pl.semaphore_signal(barrier, inc=1, device_id={"tile": partner(step)}, device_id_type=MESH)
    for side in range(2):

        @pl.when(sends[side])
        def _():
            pl.semaphore_signal(barrier, inc=1, device_id={"tile": target[side]}, device_id_type=MESH)

    loads = [
        pltpu.make_async_copy(mask_hbm, mask_ref, in_sem.at[0]),
        pltpu.make_async_copy(tk_hbm, tk_ref, in_sem.at[1]),
        pltpu.make_async_copy(tv_hbm, tv_ref, in_sem.at[2]),
        pltpu.make_async_copy(q_hbm.at[0], q_ref, in_sem.at[3]),
    ]
    for which, source in enumerate((k_hbm, v_hbm)):
        for head in range(head_count):
            cols = pl.ds(head * HEAD_DIM, HEAD_DIM)
            loads.append(
                pltpu.make_async_copy(
                    source.at[0, pl.ds(0, rows_kept), cols], own.at[head, which], in_sem.at[4 + which * head_count + head]
                )
            )
    for load in loads:
        load.start()

    def near_copy(side, head):
        return pltpu.make_async_remote_copy(
            src_ref=own.at[head],
            dst_ref=near.at[side, head],
            send_sem=near_send.at[side, head],
            recv_sem=near_recv.at[side, head],
            device_id={"tile": target[side]},
            device_id_type=MESH,
        )

    def start_near(head):
        for side in range(2):

            @pl.when(sends[side])
            def _():
                near_copy(side, head).start()

    def plane_copies(step):
        to = partner(step)
        made = []
        for which, (source, landing) in enumerate(
            (
                (packets.at[lax.rem(group + step, groups)], text.at[tile, pl.ds(group * per_source, per_source)]),
                (flags_in.at[group], flags_in.at[group]),
            )
        ):
            made.append(
                pltpu.make_async_remote_copy(
                    src_ref=source,
                    dst_ref=landing,
                    send_sem=plane_send.at[step, which],
                    recv_sem=plane_recv.at[step, which],
                    device_id={"tile": to},
                    device_id_type=MESH,
                )
            )
        return made

    def chain_copy(side, hop, owner):
        return pltpu.make_async_remote_copy(
            src_ref=text.at[owner],
            dst_ref=text.at[owner],
            send_sem=chain_send.at[side, hop],
            recv_sem=chain_recv.at[side, hop],
            device_id={"tile": target[side]},
            device_id_type=MESH,
        )

    def chain_sent(side, hop):
        owner = tile - hop if side == 0 else tile + hop
        there = owner >= 0 if side == 0 else owner < tiles
        return owner, there & sends[side]

    def chain_got(side, hop):
        owner = tile - hop - 1 if side == 0 else tile + hop + 1
        return owner, owner >= 0 if side == 0 else owner < tiles

    def start_chain(hop):
        for side in range(2):
            owner, there = chain_sent(side, hop)

            @pl.when(there)
            def _():
                chain_copy(side, hop, owner).start()

    def wait_chain(hop):
        for side in range(2):
            owner, there = chain_got(side, hop)

            @pl.when(there)
            def _():
                chain_copy(side, hop, owner).wait_recv()

    def fold(head, keys, values, keep, first):
        query = q_ref[:, head_cols(head)]
        scores = lax.dot_general(query, keys, (((1,), (1,)), ((), ())), preferred_element_type=jnp.float32)
        if keep is not None:
            scores = jnp.where(keep, scores, MASKED)
        block_top = jnp.broadcast_to(jnp.max(scores, axis=1, keepdims=True), (scores.shape[0], HEAD_DIM))
        new_top = block_top if first else jnp.maximum(top_ref[head], block_top)
        pieces = [
            jnp.exp2((scores[:, at : at + HEAD_DIM] - new_top) * EXP2_SCALE) for at in range(0, keys.shape[0], HEAD_DIM)
        ]
        part = functools.reduce(lambda a, b: a + b, pieces)
        weights = jnp.concatenate([piece.astype(jnp.bfloat16) for piece in pieces], axis=1)
        product = jnp.dot(weights, values, preferred_element_type=jnp.float32)
        if first:
            total_ref[head] = part
            summed_ref[head] = product
        else:
            scale_down = jnp.exp2((top_ref[head] - new_top) * EXP2_SCALE)
            total_ref[head] = total_ref[head] * scale_down + part
            summed_ref[head] = summed_ref[head] * scale_down + product
        top_ref[head] = new_top

    def head_cols(head):
        return slice(head * HEAD_DIM, (head + 1) * HEAD_DIM)

    def fold_near(head):
        for side in range(2):

            @pl.when(receives[side])
            def _():
                near_copy(side, head).wait_recv()
                fold(head, near[side, head, 0], near[side, head, 1], None, False)

    def fold_own(head):
        fold(head, own[head, 0], own[head, 1], None, True)

    def fold_text(blocks):
        short = -(len(blocks) * groups * text_rows) % HEAD_DIM
        fill = [jnp.zeros((short, HEAD_DIM), jnp.bfloat16)] if short else []
        lane = lax.broadcasted_iota(jnp.int32, (text_rows, HEAD_DIM), 1)
        spread = []
        for block in blocks:
            flags = text[block, flag_at]
            for source in range(groups):
                spread.append(jnp.where(lane == block * groups + source, flags, jnp.zeros_like(flags)))
        keep_row = lax.dot_general(
            jnp.ones((8, HEAD_DIM), jnp.bfloat16),
            jnp.concatenate(spread + fill, axis=0),
            (((1,), (1,)), ((), ())),
            preferred_element_type=jnp.float32,
        )[0:1, :]
        keep = jnp.broadcast_to(keep_row, (q_ref.shape[0], keep_row.shape[1])) > 0.5

        def piece(at):
            found = [text[block, source * per_source + at] for block in blocks for source in range(groups)]
            return jnp.concatenate(found + fill, axis=0)

        for head in range(head_count):
            fold(head, piece(head), piece(head_count + head), keep, False)

    def finish(head):
        total = jnp.sum(total_ref[head], axis=1, keepdims=True)
        out_ref[0, :, head_cols(head)] = (summed_ref[head] / total).astype(out_ref.dtype)

    pl.semaphore_wait(barrier, groups - 1 + has_left.astype(jnp.int32) + has_right.astype(jnp.int32))
    for load in loads[3:]:
        load.wait()
    start_near(0)

    loads[0].wait()
    row_of = lax.broadcasted_iota(jnp.int32, (text_rows, HEAD_DIM), 0)
    lane_of = lax.broadcasted_iota(jnp.int32, (text_rows, HEAD_DIM), 1)
    flags = jnp.zeros((text_rows, HEAD_DIM), jnp.float32)
    for row in range(text_rows):
        flags = jnp.where((row_of == row) & (lane_of == me), mask_ref[row].astype(jnp.float32), flags)
    flags_in[group] = flags.astype(jnp.bfloat16)
    loads[1].wait()
    loads[2].wait()
    for to in range(groups):
        for which, source in enumerate((tk_ref, tv_ref)):
            for head in range(head_count):
                at = (to * head_count + head) * HEAD_DIM
                packets[to, which * head_count + head] = source[:, at : at + HEAD_DIM]
    text[tile, pl.ds(group * per_source, per_source)] = packets[group]
    for step in range(1, groups):
        for copy in plane_copies(step):
            copy.start()
    fold_own(0)
    for step in range(1, groups):
        for copy in plane_copies(step):
            copy.wait_recv()
    text[tile, flag_at] = functools.reduce(lambda a, b: a + b, [flags_in[source] for source in range(groups)])

    start_chain(0)
    start_near(1)
    for head in range(1, head_count):
        fold_own(head)
    for hop in range(1, tiles - 1):
        wait_chain(hop - 1)
        start_chain(hop)
        if hop == 1:
            for head in range(2, head_count):
                start_near(head)
            fold_near(0)
    if tiles == 2:
        for head in range(2, head_count):
            start_near(head)
        fold_near(0)
    for head in range(1, head_count):
        fold_near(head)

    if tiles == 4:
        at_end = (tile == 0) | (tile == tiles - 1)

        @pl.when(at_end)
        def _():
            start = (tile > 0).astype(jnp.int32)
            fold_text([start + block for block in range(tiles - 1)])
            wait_chain(tiles - 2)
            fold_text([tiles - 1 - tile])

        @pl.when(jnp.logical_not(at_end))
        def _():
            fold_text(range(tiles))

    else:
        wait_chain(tiles - 2)
        fold_text(range(tiles))

    for head in range(head_count):
        finish(head)

    for step in range(1, groups):
        for copy in plane_copies(step):
            copy.wait_send()
    for side in range(2):

        @pl.when(sends[side])
        def _():
            for head in range(head_count):
                near_copy(side, head).wait_send()

        for hop in range(tiles - 1):
            owner, there = chain_sent(side, hop)

            @pl.when(there)
            def _():
                chain_copy(side, hop, owner).wait_send()


def row_shards(queries, keys, values, text_keys, text_values, text_mask):
    tokens, width = queries.shape[1:]
    head_count = width // HEAD_DIM
    count = lax.axis_size("tile")
    tiles = count // HEAD_GROUPS
    text_rows = text_keys.shape[0]
    rows_kept = (TS - TS // 4) * TS * TS
    bf16, f32 = jnp.bfloat16, jnp.float32
    dma = pltpu.SemaphoreType.DMA
    hbm = pl.BlockSpec(memory_space=pltpu.HBM)
    keys_seen = 3 * rows_kept + count * text_rows
    per_source = 2 * head_count
    return pl.pallas_call(
        functools.partial(row_kernel, count, rows_kept, head_count, text_rows),
        out_shape=pltpu.VMEM(queries.shape, bf16),
        in_specs=[hbm] * 6,
        out_specs=pl.BlockSpec(memory_space=pltpu.VMEM),
        scratch_shapes=[
            pltpu.VMEM((tokens, width), bf16),
            pltpu.VMEM((head_count, 2, rows_kept, HEAD_DIM), bf16),
            pltpu.VMEM(text_keys.shape, bf16),
            pltpu.VMEM(text_keys.shape, bf16),
            pltpu.SMEM((text_rows,), jnp.int32),
            pltpu.VMEM((HEAD_GROUPS, per_source, text_rows, HEAD_DIM), bf16),
            pltpu.VMEM((HEAD_GROUPS, text_rows, HEAD_DIM), bf16),
            pltpu.VMEM((tiles, HEAD_GROUPS * per_source + 1, text_rows, HEAD_DIM), bf16),
            pltpu.VMEM((2, head_count, 2, rows_kept, HEAD_DIM), bf16),
            pltpu.VMEM((head_count, tokens, HEAD_DIM), f32),
            pltpu.VMEM((head_count, tokens, HEAD_DIM), f32),
            pltpu.VMEM((head_count, tokens, HEAD_DIM), f32),
            dma((4 + 2 * head_count,)),
            dma((HEAD_GROUPS, 2)),
            dma((HEAD_GROUPS, 2)),
            dma((2, tiles - 1)),
            dma((2, tiles - 1)),
            dma((2, head_count)),
            dma((2, head_count)),
        ],
        compiler_params=pltpu.CompilerParams(
            collective_id=0, has_side_effects=True, vmem_limit_bytes=56 * 1024 * 1024
        ),
        cost_estimate=pl.CostEstimate(
            flops=4 * tokens * keys_seen * width,
            bytes_accessed=10 * tokens * width,
            transcendentals=tokens * keys_seen * head_count,
        ),
    )(queries, keys, values, text_keys, text_values, text_mask)


def solution(mesh):
    tiles = mesh.shape["tile"] // HEAD_GROUPS

    def shards(*blocks):
        one_row = 1 < tiles <= 4 and blocks[3].shape[0] % 16 == 0
        return (row_shards if one_row else gathered_shards)(*blocks)

    return jax.shard_map(
        shards,
        mesh=mesh,
        in_specs=(
            P(("req", "tile"), None, None),
            P(("req", "tile"), None, None),
            P(("req", "tile"), None, None),
            P(("req", "tile"), None),
            P(("req", "tile"), None),
            P(("req", "tile")),
        ),
        out_specs=P(("req", "tile"), None, None),
        check_vma=False,
    )
```

```python
import functools
import math

import jax
import jax.numpy as jnp
from jax import lax
from jax.experimental import pallas as pl
from jax.experimental.pallas import tpu as pltpu
from jax.sharding import PartitionSpec as P

MESH = pl.DeviceIdType.MESH
EXP2_SCALE = math.log2(math.e) / math.sqrt(128)

TS = 8
HEAD_DIM = 128
HEAD_GROUPS = 4


MASKED = -1e30


def passed_along(value, axis, steps):
    count = lax.axis_size(axis)
    first, last = (max(0, -steps), min(count, count - steps))
    return lax.ppermute(value, axis, [(source, source + steps) for source in range(first, last)])


def shortened(value):
    return jax.tree.map(lambda a: a.astype(jnp.bfloat16) if a.dtype == jnp.float32 else a, value)


def fold_block(running, query_heads, key_block, value_block, key_keep):
    row_top, row_total, summed = running
    head_count = query_heads.shape[1]
    key_heads = key_block.reshape(key_block.shape[0], head_count, HEAD_DIM)
    value_heads = value_block.reshape(value_block.shape[0], head_count, HEAD_DIM)
    scores = jnp.einsum("qhd,khd->hqk", query_heads, key_heads, preferred_element_type=jnp.float32)
    scores = scores * (1.0 / math.sqrt(HEAD_DIM))
    scores = jnp.where(key_keep[None, None, :], scores, MASKED)
    new_top = jnp.maximum(row_top, jnp.max(scores, axis=-1))
    scale_down = jnp.exp(row_top - new_top)
    exp_terms = jnp.where(key_keep[None, None, :], jnp.exp(scores - new_top[:, :, None]), 0.0)
    row_total = row_total * scale_down + jnp.sum(exp_terms, axis=-1)
    weights = exp_terms.astype(jnp.bfloat16)
    summed = summed * scale_down[:, :, None] + jnp.einsum(
        "hqk,khd->hqd", weights, value_heads, preferred_element_type=jnp.float32
    )
    return (new_top, row_total, summed)


def gathered_shards(queries, keys, values, text_keys, text_values, text_mask):
    tokens = queries.shape[1]
    lane_width = queries.shape[2]
    head_count = lane_width // HEAD_DIM
    query_heads = queries[0].reshape(tokens, head_count, HEAD_DIM)
    own_pair = jnp.stack([keys[0], values[0]])
    group_count = HEAD_GROUPS
    tiles_all = lax.axis_size("tile") // group_count
    grid_w = min(4, tiles_all)
    grid_h = min(4, tiles_all // grid_w)
    grid_f = tiles_all // (grid_w * grid_h)
    frames_valid = grid_f * TS - TS // 4
    my_index = lax.axis_index("tile")
    tile_id = my_index // group_count
    head_group = my_index % group_count
    w_pos = tile_id % grid_w
    h_pos = tile_id // grid_w % grid_h
    f_pos = tile_id // (grid_w * grid_h)
    local_frame = jnp.arange(tokens, dtype=jnp.int32) // (TS * TS)

    def keep_mask(off_frame, off_height, off_width):
        inside = (
            (f_pos + off_frame >= 0)
            & (f_pos + off_frame < grid_f)
            & (h_pos + off_height >= 0)
            & (h_pos + off_height < grid_h)
            & (w_pos + off_width >= 0)
            & (w_pos + off_width < grid_w)
        )
        return inside & ((f_pos + off_frame) * TS + local_frame < frames_valid)

    running = (
        jnp.full((head_count, tokens), MASKED, jnp.float32),
        jnp.zeros((head_count, tokens), jnp.float32),
        jnp.zeros((head_count, tokens, HEAD_DIM), jnp.float32),
    )
    text_flags = text_mask.astype(jnp.bfloat16)
    piece_keys = lax.dynamic_slice_in_dim(
        lax.all_gather(text_keys, "tile", axis=0, tiled=True),
        head_group * lane_width,
        lane_width,
        1,
    )
    piece_values = lax.dynamic_slice_in_dim(
        lax.all_gather(text_values, "tile", axis=0, tiled=True),
        head_group * lane_width,
        lane_width,
        1,
    )
    running = fold_block(
        running,
        query_heads,
        piece_keys,
        piece_values,
        lax.all_gather(text_flags, "tile", axis=0, tiled=True) > 0.5,
    )
    running = fold_block(running, query_heads, own_pair[0], own_pair[1], keep_mask(0, 0, 0))
    width_set = {0: own_pair}
    for off_width in (-1, 1):
        width_set[off_width] = passed_along(own_pair, "tile", -off_width * group_count)
    width_offsets = sorted(width_set)
    row_stack = jnp.stack([width_set[spot] for spot in width_offsets])
    height_set = {0: row_stack}
    if grid_h > 1:
        for off_height in (-1, 1):
            height_set[off_height] = passed_along(
                shortened(row_stack), "tile", -off_height * grid_w * group_count
            ).astype(row_stack.dtype)
    height_offsets = sorted(height_set)
    slab_stack = jnp.stack([height_set[spot] for spot in height_offsets])

    def fold_slab(state_now, slab_pairs, off_frame):
        for h_slot, off_height in enumerate(height_offsets):
            for w_slot, off_width in enumerate(width_offsets):
                if off_frame == 0 and off_height == 0 and (off_width == 0):
                    continue
                state_now = fold_block(
                    state_now,
                    query_heads,
                    slab_pairs[h_slot, w_slot, 0],
                    slab_pairs[h_slot, w_slot, 1],
                    keep_mask(off_frame, off_height, off_width),
                )
        return state_now

    running = fold_slab(running, slab_stack, 0)
    if grid_f > 1:
        for off_frame in (-1, 1):
            got_slab = passed_along(
                shortened(slab_stack), "tile", -off_frame * grid_h * grid_w * group_count
            ).astype(slab_stack.dtype)
            running = fold_slab(running, got_slab, off_frame)
    row_top, row_total, summed = running
    result = summed / row_total[:, :, None]
    result = jnp.transpose(result, (1, 0, 2)).reshape(tokens, lane_width)
    return result.astype(jnp.bfloat16)[None]


def row_kernel(
    count, rows_kept, head_count, text_rows,
    q_hbm, k_hbm, v_hbm, tk_hbm, tv_hbm, mask_hbm, out_ref,
    q_ref, own, tk_ref, tv_ref, mask_ref, packets, flags_in, text, near,
    top_ref, total_ref, summed_ref,
    in_sem, plane_send, plane_recv, chain_send, chain_recv, near_send, near_recv,
):
    groups = HEAD_GROUPS
    tiles = count // groups
    per_source = 2 * head_count
    flag_at = groups * per_source
    me = lax.axis_index("tile")
    tile = me // groups
    group = lax.rem(me, groups)
    first_here = tile * groups
    has_left = tile > 0
    has_right = tile < tiles - 1
    target = (me + groups, me - groups)
    sends = (has_right, has_left)
    receives = (has_left, has_right)

    def partner(step):
        return first_here + lax.rem(group + step, groups)

    barrier = pltpu.get_barrier_semaphore()
    for step in range(1, groups):
        pl.semaphore_signal(barrier, inc=1, device_id={"tile": partner(step)}, device_id_type=MESH)
    for side in range(2):

        @pl.when(sends[side])
        def _():
            pl.semaphore_signal(barrier, inc=1, device_id={"tile": target[side]}, device_id_type=MESH)

    loads = [
        pltpu.make_async_copy(mask_hbm, mask_ref, in_sem.at[0]),
        pltpu.make_async_copy(tk_hbm, tk_ref, in_sem.at[1]),
        pltpu.make_async_copy(tv_hbm, tv_ref, in_sem.at[2]),
        pltpu.make_async_copy(q_hbm.at[0], q_ref, in_sem.at[3]),
    ]
    for which, source in enumerate((k_hbm, v_hbm)):
        for head in range(head_count):
            cols = pl.ds(head * HEAD_DIM, HEAD_DIM)
            loads.append(
                pltpu.make_async_copy(
                    source.at[0, pl.ds(0, rows_kept), cols], own.at[head, which], in_sem.at[4 + which * head_count + head]
                )
            )
    for load in loads:
        load.start()

    def near_copy(side, head):
        return pltpu.make_async_remote_copy(
            src_ref=own.at[head],
            dst_ref=near.at[side, head],
            send_sem=near_send.at[side, head],
            recv_sem=near_recv.at[side, head],
            device_id={"tile": target[side]},
            device_id_type=MESH,
        )

    def start_near(head):
        for side in range(2):

            @pl.when(sends[side])
            def _():
                near_copy(side, head).start()

    def plane_copies(step):
        to = partner(step)
        made = []
        for which, (source, landing) in enumerate(
            (
                (packets.at[lax.rem(group + step, groups)], text.at[tile, pl.ds(group * per_source, per_source)]),
                (flags_in.at[group], flags_in.at[group]),
            )
        ):
            made.append(
                pltpu.make_async_remote_copy(
                    src_ref=source,
                    dst_ref=landing,
                    send_sem=plane_send.at[step, which],
                    recv_sem=plane_recv.at[step, which],
                    device_id={"tile": to},
                    device_id_type=MESH,
                )
            )
        return made

    def chain_copy(side, hop, owner):
        return pltpu.make_async_remote_copy(
            src_ref=text.at[owner],
            dst_ref=text.at[owner],
            send_sem=chain_send.at[side, hop],
            recv_sem=chain_recv.at[side, hop],
            device_id={"tile": target[side]},
            device_id_type=MESH,
        )

    def chain_sent(side, hop):
        owner = tile - hop if side == 0 else tile + hop
        there = owner >= 0 if side == 0 else owner < tiles
        return owner, there & sends[side]

    def chain_got(side, hop):
        owner = tile - hop - 1 if side == 0 else tile + hop + 1
        return owner, owner >= 0 if side == 0 else owner < tiles

    def start_chain(hop):
        for side in range(2):
            owner, there = chain_sent(side, hop)

            @pl.when(there)
            def _():
                chain_copy(side, hop, owner).start()

    def wait_chain(hop):
        for side in range(2):
            owner, there = chain_got(side, hop)

            @pl.when(there)
            def _():
                chain_copy(side, hop, owner).wait_recv()

    def fold(head, keys, values, keep, first):
        query = q_ref[:, head_cols(head)]
        scores = lax.dot_general(query, keys, (((1,), (1,)), ((), ())), preferred_element_type=jnp.float32)
        if keep is not None:
            scores = jnp.where(keep, scores, MASKED)
        block_top = jnp.broadcast_to(jnp.max(scores, axis=1, keepdims=True), (scores.shape[0], HEAD_DIM))
        new_top = block_top if first else jnp.maximum(top_ref[head], block_top)
        pieces = [
            jnp.exp2((scores[:, at : at + HEAD_DIM] - new_top) * EXP2_SCALE) for at in range(0, keys.shape[0], HEAD_DIM)
        ]
        part = functools.reduce(lambda a, b: a + b, pieces)
        weights = jnp.concatenate([piece.astype(jnp.bfloat16) for piece in pieces], axis=1)
        product = jnp.dot(weights, values, preferred_element_type=jnp.float32)
        if first:
            total_ref[head] = part
            summed_ref[head] = product
        else:
            scale_down = jnp.exp2((top_ref[head] - new_top) * EXP2_SCALE)
            total_ref[head] = total_ref[head] * scale_down + part
            summed_ref[head] = summed_ref[head] * scale_down + product
        top_ref[head] = new_top

    def head_cols(head):
        return slice(head * HEAD_DIM, (head + 1) * HEAD_DIM)

    def fold_near(head):
        for side in range(2):

            @pl.when(receives[side])
            def _():
                near_copy(side, head).wait_recv()
                fold(head, near[side, head, 0], near[side, head, 1], None, False)

    def fold_own(head):
        fold(head, own[head, 0], own[head, 1], None, True)

    def fold_text(blocks, done=()):
        short = -(len(blocks) * groups * text_rows) % HEAD_DIM
        fill = [jnp.zeros((short, HEAD_DIM), jnp.bfloat16)] if short else []
        lane = lax.broadcasted_iota(jnp.int32, (text_rows, HEAD_DIM), 1)
        spread = []
        for block in blocks:
            flags = text[block, flag_at]
            for source in range(groups):
                spread.append(jnp.where(lane == block * groups + source, flags, jnp.zeros_like(flags)))
        keep_row = lax.dot_general(
            jnp.ones((8, HEAD_DIM), jnp.bfloat16),
            jnp.concatenate(spread + fill, axis=0),
            (((1,), (1,)), ((), ())),
            preferred_element_type=jnp.float32,
        )[0:1, :]
        keep = jnp.broadcast_to(keep_row, (q_ref.shape[0], keep_row.shape[1])) > 0.5

        def piece(at):
            found = [text[block, source * per_source + at] for block in blocks for source in range(groups)]
            return jnp.concatenate(found + fill, axis=0)

        for head in range(head_count):
            fold(head, piece(head), piece(head_count + head), keep, False)
            if head in done:
                finish(head)

    def finish(head):
        total = jnp.sum(total_ref[head], axis=1, keepdims=True)
        out_ref[0, :, head_cols(head)] = (summed_ref[head] / total).astype(out_ref.dtype)

    pl.semaphore_wait(barrier, groups - 1 + has_left.astype(jnp.int32) + has_right.astype(jnp.int32))
    for load in loads[3:]:
        load.wait()
    start_near(0)

    loads[0].wait()
    row_of = lax.broadcasted_iota(jnp.int32, (text_rows, HEAD_DIM), 0)
    lane_of = lax.broadcasted_iota(jnp.int32, (text_rows, HEAD_DIM), 1)
    flags = jnp.zeros((text_rows, HEAD_DIM), jnp.float32)
    for row in range(text_rows):
        flags = jnp.where((row_of == row) & (lane_of == me), mask_ref[row].astype(jnp.float32), flags)
    flags_in[group] = flags.astype(jnp.bfloat16)
    loads[1].wait()
    loads[2].wait()
    for to in range(groups):
        for which, source in enumerate((tk_ref, tv_ref)):
            for head in range(head_count):
                at = (to * head_count + head) * HEAD_DIM
                packets[to, which * head_count + head] = source[:, at : at + HEAD_DIM]
    text[tile, pl.ds(group * per_source, per_source)] = packets[group]
    for step in range(1, groups):
        for copy in plane_copies(step):
            copy.start()
    fold_own(0)
    for step in range(1, groups):
        for copy in plane_copies(step):
            copy.wait_recv()
    text[tile, flag_at] = functools.reduce(lambda a, b: a + b, [flags_in[source] for source in range(groups)])

    start_chain(0)
    start_near(1)
    for head in range(1, head_count):
        fold_own(head)
    for hop in range(1, tiles - 1):
        wait_chain(hop - 1)
        start_chain(hop)
        if hop == 1:
            for head in range(2, head_count):
                start_near(head)
            fold_near(0)
    if tiles == 2:
        for head in range(2, head_count):
            start_near(head)
        fold_near(0)
    last = head_count - 1
    for head in range(1, last):
        fold_near(head)

    if tiles == 4:
        at_end = (tile == 0) | (tile == tiles - 1)
        inner = jnp.logical_not(at_end)

        @pl.when(at_end)
        def _():
            start = (tile > 0).astype(jnp.int32)
            fold_text([start + block for block in range(tiles - 1)])

        @pl.when(inner)
        def _():
            fold_text(range(tiles), range(last))

        fold_near(last)

        @pl.when(at_end)
        def _():
            wait_chain(tiles - 2)
            fold_text([tiles - 1 - tile], range(head_count))

        @pl.when(inner)
        def _():
            finish(last)

    else:
        wait_chain(tiles - 2)
        fold_text(range(tiles), range(last))
        fold_near(last)
        finish(last)

    for step in range(1, groups):
        for copy in plane_copies(step):
            copy.wait_send()
    for side in range(2):

        @pl.when(sends[side])
        def _():
            for head in range(head_count):
                near_copy(side, head).wait_send()

        for hop in range(tiles - 1):
            owner, there = chain_sent(side, hop)

            @pl.when(there)
            def _():
                chain_copy(side, hop, owner).wait_send()


def row_shards(queries, keys, values, text_keys, text_values, text_mask):
    tokens, width = queries.shape[1:]
    head_count = width // HEAD_DIM
    count = lax.axis_size("tile")
    tiles = count // HEAD_GROUPS
    text_rows = text_keys.shape[0]
    rows_kept = (TS - TS // 4) * TS * TS
    bf16, f32 = jnp.bfloat16, jnp.float32
    dma = pltpu.SemaphoreType.DMA
    hbm = pl.BlockSpec(memory_space=pltpu.HBM)
    keys_seen = 3 * rows_kept + count * text_rows
    per_source = 2 * head_count
    return pl.pallas_call(
        functools.partial(row_kernel, count, rows_kept, head_count, text_rows),
        out_shape=pltpu.VMEM(queries.shape, bf16),
        in_specs=[hbm] * 6,
        out_specs=pl.BlockSpec(memory_space=pltpu.VMEM),
        scratch_shapes=[
            pltpu.VMEM((tokens, width), bf16),
            pltpu.VMEM((head_count, 2, rows_kept, HEAD_DIM), bf16),
            pltpu.VMEM(text_keys.shape, bf16),
            pltpu.VMEM(text_keys.shape, bf16),
            pltpu.SMEM((text_rows,), jnp.int32),
            pltpu.VMEM((HEAD_GROUPS, per_source, text_rows, HEAD_DIM), bf16),
            pltpu.VMEM((HEAD_GROUPS, text_rows, HEAD_DIM), bf16),
            pltpu.VMEM((tiles, HEAD_GROUPS * per_source + 1, text_rows, HEAD_DIM), bf16),
            pltpu.VMEM((2, head_count, 2, rows_kept, HEAD_DIM), bf16),
            pltpu.VMEM((head_count, tokens, HEAD_DIM), f32),
            pltpu.VMEM((head_count, tokens, HEAD_DIM), f32),
            pltpu.VMEM((head_count, tokens, HEAD_DIM), f32),
            dma((4 + 2 * head_count,)),
            dma((HEAD_GROUPS, 2)),
            dma((HEAD_GROUPS, 2)),
            dma((2, tiles - 1)),
            dma((2, tiles - 1)),
            dma((2, head_count)),
            dma((2, head_count)),
        ],
        compiler_params=pltpu.CompilerParams(
            collective_id=0, has_side_effects=True, vmem_limit_bytes=56 * 1024 * 1024
        ),
        cost_estimate=pl.CostEstimate(
            flops=4 * tokens * keys_seen * width,
            bytes_accessed=10 * tokens * width,
            transcendentals=tokens * keys_seen * head_count,
        ),
    )(queries, keys, values, text_keys, text_values, text_mask)


def solution(mesh):
    tiles = mesh.shape["tile"] // HEAD_GROUPS

    def shards(*blocks):
        one_row = 1 < tiles <= 4 and blocks[3].shape[0] % 16 == 0
        return (row_shards if one_row else gathered_shards)(*blocks)

    return jax.shard_map(
        shards,
        mesh=mesh,
        in_specs=(
            P(("req", "tile"), None, None),
            P(("req", "tile"), None, None),
            P(("req", "tile"), None, None),
            P(("req", "tile"), None),
            P(("req", "tile"), None),
            P(("req", "tile")),
        ),
        out_specs=P(("req", "tile"), None, None),
        check_vma=False,
    )
```

```python
import functools
import math

import jax
import jax.numpy as jnp
from jax import lax
from jax.experimental import pallas as pl
from jax.experimental.pallas import tpu as pltpu
from jax.sharding import PartitionSpec as P

MESH = pl.DeviceIdType.MESH
EXP2_SCALE = math.log2(math.e) / math.sqrt(128)

TS = 8
HEAD_DIM = 128
HEAD_GROUPS = 4


MASKED = -1e30


def passed_along(value, axis, steps):
    count = lax.axis_size(axis)
    first, last = (max(0, -steps), min(count, count - steps))
    return lax.ppermute(value, axis, [(source, source + steps) for source in range(first, last)])


def shortened(value):
    return jax.tree.map(lambda a: a.astype(jnp.bfloat16) if a.dtype == jnp.float32 else a, value)


def fold_block(running, query_heads, key_block, value_block, key_keep):
    row_top, row_total, summed = running
    head_count = query_heads.shape[1]
    key_heads = key_block.reshape(key_block.shape[0], head_count, HEAD_DIM)
    value_heads = value_block.reshape(value_block.shape[0], head_count, HEAD_DIM)
    scores = jnp.einsum("qhd,khd->hqk", query_heads, key_heads, preferred_element_type=jnp.float32)
    scores = scores * (1.0 / math.sqrt(HEAD_DIM))
    scores = jnp.where(key_keep[None, None, :], scores, MASKED)
    new_top = jnp.maximum(row_top, jnp.max(scores, axis=-1))
    scale_down = jnp.exp(row_top - new_top)
    exp_terms = jnp.where(key_keep[None, None, :], jnp.exp(scores - new_top[:, :, None]), 0.0)
    row_total = row_total * scale_down + jnp.sum(exp_terms, axis=-1)
    weights = exp_terms.astype(jnp.bfloat16)
    summed = summed * scale_down[:, :, None] + jnp.einsum(
        "hqk,khd->hqd", weights, value_heads, preferred_element_type=jnp.float32
    )
    return (new_top, row_total, summed)


def gathered_shards(queries, keys, values, text_keys, text_values, text_mask):
    tokens = queries.shape[1]
    lane_width = queries.shape[2]
    head_count = lane_width // HEAD_DIM
    query_heads = queries[0].reshape(tokens, head_count, HEAD_DIM)
    own_pair = jnp.stack([keys[0], values[0]])
    group_count = HEAD_GROUPS
    tiles_all = lax.axis_size("tile") // group_count
    grid_w = min(4, tiles_all)
    grid_h = min(4, tiles_all // grid_w)
    grid_f = tiles_all // (grid_w * grid_h)
    frames_valid = grid_f * TS - TS // 4
    my_index = lax.axis_index("tile")
    tile_id = my_index // group_count
    head_group = my_index % group_count
    w_pos = tile_id % grid_w
    h_pos = tile_id // grid_w % grid_h
    f_pos = tile_id // (grid_w * grid_h)
    local_frame = jnp.arange(tokens, dtype=jnp.int32) // (TS * TS)

    def keep_mask(off_frame, off_height, off_width):
        inside = (
            (f_pos + off_frame >= 0)
            & (f_pos + off_frame < grid_f)
            & (h_pos + off_height >= 0)
            & (h_pos + off_height < grid_h)
            & (w_pos + off_width >= 0)
            & (w_pos + off_width < grid_w)
        )
        return inside & ((f_pos + off_frame) * TS + local_frame < frames_valid)

    running = (
        jnp.full((head_count, tokens), MASKED, jnp.float32),
        jnp.zeros((head_count, tokens), jnp.float32),
        jnp.zeros((head_count, tokens, HEAD_DIM), jnp.float32),
    )
    text_flags = text_mask.astype(jnp.bfloat16)
    piece_keys = lax.dynamic_slice_in_dim(
        lax.all_gather(text_keys, "tile", axis=0, tiled=True),
        head_group * lane_width,
        lane_width,
        1,
    )
    piece_values = lax.dynamic_slice_in_dim(
        lax.all_gather(text_values, "tile", axis=0, tiled=True),
        head_group * lane_width,
        lane_width,
        1,
    )
    running = fold_block(
        running,
        query_heads,
        piece_keys,
        piece_values,
        lax.all_gather(text_flags, "tile", axis=0, tiled=True) > 0.5,
    )
    running = fold_block(running, query_heads, own_pair[0], own_pair[1], keep_mask(0, 0, 0))
    width_set = {0: own_pair}
    for off_width in (-1, 1):
        width_set[off_width] = passed_along(own_pair, "tile", -off_width * group_count)
    width_offsets = sorted(width_set)
    row_stack = jnp.stack([width_set[spot] for spot in width_offsets])
    height_set = {0: row_stack}
    if grid_h > 1:
        for off_height in (-1, 1):
            height_set[off_height] = passed_along(
                shortened(row_stack), "tile", -off_height * grid_w * group_count
            ).astype(row_stack.dtype)
    height_offsets = sorted(height_set)
    slab_stack = jnp.stack([height_set[spot] for spot in height_offsets])

    def fold_slab(state_now, slab_pairs, off_frame):
        for h_slot, off_height in enumerate(height_offsets):
            for w_slot, off_width in enumerate(width_offsets):
                if off_frame == 0 and off_height == 0 and (off_width == 0):
                    continue
                state_now = fold_block(
                    state_now,
                    query_heads,
                    slab_pairs[h_slot, w_slot, 0],
                    slab_pairs[h_slot, w_slot, 1],
                    keep_mask(off_frame, off_height, off_width),
                )
        return state_now

    running = fold_slab(running, slab_stack, 0)
    if grid_f > 1:
        for off_frame in (-1, 1):
            got_slab = passed_along(
                shortened(slab_stack), "tile", -off_frame * grid_h * grid_w * group_count
            ).astype(slab_stack.dtype)
            running = fold_slab(running, got_slab, off_frame)
    row_top, row_total, summed = running
    result = summed / row_total[:, :, None]
    result = jnp.transpose(result, (1, 0, 2)).reshape(tokens, lane_width)
    return result.astype(jnp.bfloat16)[None]


def row_kernel(
    count, rows_kept, head_count, text_rows,
    q_hbm, k_hbm, v_hbm, tk_hbm, tv_hbm, mask_hbm, out_ref,
    q_ref, own, tk_ref, tv_ref, mask_ref, packets, flags_in, text, near,
    top_ref, total_ref, summed_ref,
    in_sem, plane_send, plane_recv, chain_send, chain_recv, near_send, near_recv,
):
    groups = HEAD_GROUPS
    tiles = count // groups
    per_source = 2 * head_count
    flag_at = groups * per_source
    me = lax.axis_index("tile")
    tile = me // groups
    group = lax.rem(me, groups)
    first_here = tile * groups
    has_left = tile > 0
    has_right = tile < tiles - 1
    target = (me + groups, me - groups)
    sends = (has_right, has_left)
    receives = (has_left, has_right)

    def partner(step):
        return first_here + lax.rem(group + step, groups)

    barrier = pltpu.get_barrier_semaphore()
    for step in range(1, groups):
        pl.semaphore_signal(barrier, inc=1, device_id={"tile": partner(step)}, device_id_type=MESH)
    for side in range(2):

        @pl.when(sends[side])
        def _():
            pl.semaphore_signal(barrier, inc=1, device_id={"tile": target[side]}, device_id_type=MESH)

    loads = [
        pltpu.make_async_copy(mask_hbm, mask_ref, in_sem.at[0]),
        pltpu.make_async_copy(tk_hbm, tk_ref, in_sem.at[1]),
        pltpu.make_async_copy(tv_hbm, tv_ref, in_sem.at[2]),
        pltpu.make_async_copy(q_hbm.at[0], q_ref, in_sem.at[3]),
    ]
    for which, source in enumerate((k_hbm, v_hbm)):
        for head in range(head_count):
            cols = pl.ds(head * HEAD_DIM, HEAD_DIM)
            loads.append(
                pltpu.make_async_copy(
                    source.at[0, pl.ds(0, rows_kept), cols], own.at[head, which], in_sem.at[4 + which * head_count + head]
                )
            )
    for load in loads:
        load.start()

    def near_copy(side, head):
        return pltpu.make_async_remote_copy(
            src_ref=own.at[head],
            dst_ref=near.at[side, head],
            send_sem=near_send.at[side, head],
            recv_sem=near_recv.at[side, head],
            device_id={"tile": target[side]},
            device_id_type=MESH,
        )

    def start_near(head):
        for side in range(2):

            @pl.when(sends[side])
            def _():
                near_copy(side, head).start()

    def plane_copies(step):
        to = partner(step)
        made = []
        for which, (source, landing) in enumerate(
            (
                (packets.at[lax.rem(group + step, groups)], text.at[tile, pl.ds(group * per_source, per_source)]),
                (flags_in.at[group], flags_in.at[group]),
            )
        ):
            made.append(
                pltpu.make_async_remote_copy(
                    src_ref=source,
                    dst_ref=landing,
                    send_sem=plane_send.at[step, which],
                    recv_sem=plane_recv.at[step, which],
                    device_id={"tile": to},
                    device_id_type=MESH,
                )
            )
        return made

    def chain_copy(side, hop, owner):
        return pltpu.make_async_remote_copy(
            src_ref=text.at[owner],
            dst_ref=text.at[owner],
            send_sem=chain_send.at[side, hop],
            recv_sem=chain_recv.at[side, hop],
            device_id={"tile": target[side]},
            device_id_type=MESH,
        )

    def chain_sent(side, hop):
        owner = tile - hop if side == 0 else tile + hop
        there = owner >= 0 if side == 0 else owner < tiles
        return owner, there & sends[side]

    def chain_got(side, hop):
        owner = tile - hop - 1 if side == 0 else tile + hop + 1
        return owner, owner >= 0 if side == 0 else owner < tiles

    def start_chain(hop):
        for side in range(2):
            owner, there = chain_sent(side, hop)

            @pl.when(there)
            def _():
                chain_copy(side, hop, owner).start()

    def wait_chain(hop):
        for side in range(2):
            owner, there = chain_got(side, hop)

            @pl.when(there)
            def _():
                chain_copy(side, hop, owner).wait_recv()

    def fold(head, keys, values, keep, first):
        query = q_ref[:, head_cols(head)]
        scores = lax.dot_general(query, keys, (((1,), (1,)), ((), ())), preferred_element_type=jnp.float32)
        if keep is not None:
            scores = jnp.where(keep, scores, MASKED)
        block_top = jnp.broadcast_to(jnp.max(scores, axis=1, keepdims=True), (scores.shape[0], HEAD_DIM))
        new_top = block_top if first else jnp.maximum(top_ref[head], block_top)
        pieces = [
            jnp.exp2((scores[:, at : at + HEAD_DIM] - new_top) * EXP2_SCALE) for at in range(0, keys.shape[0], HEAD_DIM)
        ]
        part = functools.reduce(lambda a, b: a + b, pieces)
        weights = jnp.concatenate([piece.astype(jnp.bfloat16) for piece in pieces], axis=1)
        product = jnp.dot(weights, values, preferred_element_type=jnp.float32)
        if first:
            total_ref[head] = part
            summed_ref[head] = product
        else:
            scale_down = jnp.exp2((top_ref[head] - new_top) * EXP2_SCALE)
            total_ref[head] = total_ref[head] * scale_down + part
            summed_ref[head] = summed_ref[head] * scale_down + product
        top_ref[head] = new_top

    def head_cols(head):
        return slice(head * HEAD_DIM, (head + 1) * HEAD_DIM)

    def fold_near(head):
        for side in range(2):

            @pl.when(receives[side])
            def _():
                near_copy(side, head).wait_recv()
                fold(head, near[side, head, 0], near[side, head, 1], None, False)

    def fold_own(head):
        fold(head, own[head, 0], own[head, 1], None, True)

    def fold_text(blocks, done=()):
        short = -(len(blocks) * groups * text_rows) % HEAD_DIM
        fill = [jnp.zeros((short, HEAD_DIM), jnp.bfloat16)] if short else []
        lane = lax.broadcasted_iota(jnp.int32, (text_rows, HEAD_DIM), 1)
        spread = []
        for block in blocks:
            flags = text[block, flag_at]
            for source in range(groups):
                spread.append(jnp.where(lane == block * groups + source, flags, jnp.zeros_like(flags)))
        keep_row = lax.dot_general(
            jnp.ones((8, HEAD_DIM), jnp.bfloat16),
            jnp.concatenate(spread + fill, axis=0),
            (((1,), (1,)), ((), ())),
            preferred_element_type=jnp.float32,
        )[0:1, :]
        keep = jnp.broadcast_to(keep_row, (q_ref.shape[0], keep_row.shape[1])) > 0.5

        def piece(at):
            found = [text[block, source * per_source + at] for block in blocks for source in range(groups)]
            return jnp.concatenate(found + fill, axis=0)

        for head in range(head_count):
            fold(head, piece(head), piece(head_count + head), keep, False)
            if head in done:
                finish(head)

    def finish(head):
        total = jnp.sum(total_ref[head], axis=1, keepdims=True)
        out_ref[0, :, head_cols(head)] = (summed_ref[head] / total).astype(out_ref.dtype)

    pl.semaphore_wait(barrier, groups - 1 + has_left.astype(jnp.int32) + has_right.astype(jnp.int32))
    for load in loads[3:]:
        load.wait()
    start_near(0)

    loads[0].wait()
    row_of = lax.broadcasted_iota(jnp.int32, (text_rows, HEAD_DIM), 0)
    lane_of = lax.broadcasted_iota(jnp.int32, (text_rows, HEAD_DIM), 1)
    flags = jnp.zeros((text_rows, HEAD_DIM), jnp.float32)
    for row in range(text_rows):
        flags = jnp.where((row_of == row) & (lane_of == me), mask_ref[row].astype(jnp.float32), flags)
    flags_in[group] = flags.astype(jnp.bfloat16)
    loads[1].wait()
    loads[2].wait()
    for to in range(groups):
        for which, source in enumerate((tk_ref, tv_ref)):
            for head in range(head_count):
                at = (to * head_count + head) * HEAD_DIM
                packets[to, which * head_count + head] = source[:, at : at + HEAD_DIM]
    text[tile, pl.ds(group * per_source, per_source)] = packets[group]
    for step in range(1, groups):
        for copy in plane_copies(step):
            copy.start()
    fold_own(0)
    for step in range(1, groups):
        for copy in plane_copies(step):
            copy.wait_recv()
    text[tile, flag_at] = functools.reduce(lambda a, b: a + b, [flags_in[source] for source in range(groups)])

    start_chain(0)
    start_near(1)
    for head in range(1, head_count):
        fold_own(head)
    for hop in range(1, tiles - 1):
        wait_chain(hop - 1)
        start_chain(hop)
        if hop == tiles - 2:
            for head in range(2, head_count):
                start_near(head)
        if hop == 1:
            fold_near(0)
    if tiles == 2:
        for head in range(2, head_count):
            start_near(head)
        fold_near(0)
    last = head_count - 1
    for head in range(1, last):
        fold_near(head)

    if tiles == 4:
        at_end = (tile == 0) | (tile == tiles - 1)
        inner = jnp.logical_not(at_end)

        @pl.when(at_end)
        def _():
            start = (tile > 0).astype(jnp.int32)
            fold_text([start + block for block in range(tiles - 1)])

        @pl.when(inner)
        def _():
            fold_text(range(tiles), range(last))

        fold_near(last)

        @pl.when(at_end)
        def _():
            wait_chain(tiles - 2)
            fold_text([tiles - 1 - tile], range(head_count))

        @pl.when(inner)
        def _():
            finish(last)

    else:
        wait_chain(tiles - 2)
        fold_text(range(tiles), range(last))
        fold_near(last)
        finish(last)

    for step in range(1, groups):
        for copy in plane_copies(step):
            copy.wait_send()
    for side in range(2):

        @pl.when(sends[side])
        def _():
            for head in range(head_count):
                near_copy(side, head).wait_send()

        for hop in range(tiles - 1):
            owner, there = chain_sent(side, hop)

            @pl.when(there)
            def _():
                chain_copy(side, hop, owner).wait_send()


def row_shards(queries, keys, values, text_keys, text_values, text_mask):
    tokens, width = queries.shape[1:]
    head_count = width // HEAD_DIM
    count = lax.axis_size("tile")
    tiles = count // HEAD_GROUPS
    text_rows = text_keys.shape[0]
    rows_kept = (TS - TS // 4) * TS * TS
    bf16, f32 = jnp.bfloat16, jnp.float32
    dma = pltpu.SemaphoreType.DMA
    hbm = pl.BlockSpec(memory_space=pltpu.HBM)
    keys_seen = 3 * rows_kept + count * text_rows
    per_source = 2 * head_count
    return pl.pallas_call(
        functools.partial(row_kernel, count, rows_kept, head_count, text_rows),
        out_shape=pltpu.VMEM(queries.shape, bf16),
        in_specs=[hbm] * 6,
        out_specs=pl.BlockSpec(memory_space=pltpu.VMEM),
        scratch_shapes=[
            pltpu.VMEM((tokens, width), bf16),
            pltpu.VMEM((head_count, 2, rows_kept, HEAD_DIM), bf16),
            pltpu.VMEM(text_keys.shape, bf16),
            pltpu.VMEM(text_keys.shape, bf16),
            pltpu.SMEM((text_rows,), jnp.int32),
            pltpu.VMEM((HEAD_GROUPS, per_source, text_rows, HEAD_DIM), bf16),
            pltpu.VMEM((HEAD_GROUPS, text_rows, HEAD_DIM), bf16),
            pltpu.VMEM((tiles, HEAD_GROUPS * per_source + 1, text_rows, HEAD_DIM), bf16),
            pltpu.VMEM((2, head_count, 2, rows_kept, HEAD_DIM), bf16),
            pltpu.VMEM((head_count, tokens, HEAD_DIM), f32),
            pltpu.VMEM((head_count, tokens, HEAD_DIM), f32),
            pltpu.VMEM((head_count, tokens, HEAD_DIM), f32),
            dma((4 + 2 * head_count,)),
            dma((HEAD_GROUPS, 2)),
            dma((HEAD_GROUPS, 2)),
            dma((2, tiles - 1)),
            dma((2, tiles - 1)),
            dma((2, head_count)),
            dma((2, head_count)),
        ],
        compiler_params=pltpu.CompilerParams(
            collective_id=0, has_side_effects=True, vmem_limit_bytes=56 * 1024 * 1024
        ),
        cost_estimate=pl.CostEstimate(
            flops=4 * tokens * keys_seen * width,
            bytes_accessed=10 * tokens * width,
            transcendentals=tokens * keys_seen * head_count,
        ),
    )(queries, keys, values, text_keys, text_values, text_mask)


def solution(mesh):
    tiles = mesh.shape["tile"] // HEAD_GROUPS

    def shards(*blocks):
        one_row = 1 < tiles <= 4 and blocks[3].shape[0] % 16 == 0
        return (row_shards if one_row else gathered_shards)(*blocks)

    return jax.shard_map(
        shards,
        mesh=mesh,
        in_specs=(
            P(("req", "tile"), None, None),
            P(("req", "tile"), None, None),
            P(("req", "tile"), None, None),
            P(("req", "tile"), None),
            P(("req", "tile"), None),
            P(("req", "tile")),
        ),
        out_specs=P(("req", "tile"), None, None),
        check_vma=False,
    )
```
